32 devices in a mesh: dp: 4 (over y, core), expert: 8 (over z, x).
Axes of the slice: x: 2, y: 2, z: 4, core: 2. Of those that a mesh axis runs over, the one named last changes fastest.
Arguments:
- hidden_in: bfloat16 [8, 4, 640, 1024], P('expert', 'dp'), may hold values from -6 to 6
- down_weight: bfloat16 [8, 1024, 3584], P('expert'), may hold values from -0.1875 to 0.1875
- routes: int32 [4096, 4], P(('dp', 'expert')), may hold values from 0 to 7, all different within a row; in each aligned block of 128 rows (0 to 127, 128 to 255, ...) at most 80 rows name the same one
- gate_prob: float32 [4096, 4], P(('dp', 'expert')), may hold values from 0.05 to 1
- cotangent: bfloat16 [4096, 3584], P(('dp', 'expert')), may hold values from -0.59765625 to 0.59765625
Outputs:
- combined: bfloat16 [4096, 3584], P(('dp', 'expert'))
- gate_grad: float32 [4096, 4], P(('dp', 'expert'))
- hidden_grad: bfloat16 [8, 4, 640, 1024], P('expert', 'dp')
- weight_grad: bfloat16 [8, 1024, 3584], P('expert', 'dp')
The draws below stay inside these ranges and needn't reach their ends.
Inputs may be any that keep to these rules, and one draw needn't show every extreme that they name: `routes`: each row names 4 different experts. Within the rows of one device (aligned blocks of 128 rows) no expert is named by more than 80 rows, a bound that some block reaches.
All inputs are finite; a program needn't handle non-finite values.
Results may differ from the reference program's by a relative error of at most 0.017.
Values may be sent and summed in bfloat16 or wider, within the bound.
No kernel may reach another device: no remote copies, remote signals or barrier semaphores. Data moves between devices by JAX's collectives and lax.ppermute only.
A program may use at most 128 MiB of HBM per device.

```python
import math
import jax
import jax.numpy as jnp
import numpy as np
from jax import lax

D = 3584
FF = 1024
TOPK = 4
TOK_DEV = 128
EXPERTS = 8
CAP = 80
ROWS = 640
TOKENS = 4096
N_DP = 4
N_EXPERT = 8


def shard_levels(own_key, extent, shards, smallest, high):
    gain = 1.0
    for position, blocks in shards:
        steps = jax.random.uniform(jax.random.fold_in(jax.random.fold_in(own_key, 6), position), (blocks,), jnp.float32, smallest / len(shards), high / len(shards))
        gain = gain * jnp.repeat(jnp.exp(steps), extent[position] // blocks).reshape((-1,) + (1,) * (len(extent) - 1 - position))
    return gain


def deal_out(stream_key, own, number, rows, amount, top, limit, slope):
    sequence = jax.random.permutation(stream_key, amount)
    crowded, common = portions_of(amount, rows * top, limit, slope, True), portions_of(amount, rows * top, limit, slope, False)
    places = jnp.arange(amount)

    def named(tallies, turn):
        used = int((tallies > 0).sum())
        fixed = max(1, used // 4)
        shifted = fixed + (places - fixed + turn * (used - fixed)) % max(1, amount - fixed)
        return jnp.zeros((amount,), jnp.int32).at[sequence[jnp.where(places < fixed, places, shifted)]].set(jnp.asarray(tallies, jnp.int32))

    tallies = jnp.where(number % 4 == 0, named(crowded, number // 4), named(common, number - number // 4 - 1))
    mixed = jax.random.permutation(jax.random.fold_in(own, 3), amount)
    donor, sink = mixed[0:amount // 2 * 2:2], mixed[1:amount // 2 * 2:2]
    slack = jnp.minimum(tallies[donor] - 1, limit - tallies[sink]) // 2
    slack = jnp.where((donor == sequence[0]) | (sink == sequence[0]) | (tallies[sink] == 0), 0, jnp.maximum(slack, 0))
    shifted = jax.random.randint(jax.random.fold_in(own, 4), (amount // 2,), 0, 1 << 20) % (slack + 1)
    tallies = tallies.at[donor].add(-shifted).at[sink].add(shifted)
    members = jnp.searchsorted(jnp.cumsum(tallies), jnp.arange(rows * top), side="right").astype(jnp.int32)
    listing = members.reshape(top, rows).T
    listing = listing[jax.random.permutation(jax.random.fold_in(own, 1), rows)]
    turn = jax.random.randint(jax.random.fold_in(own, 2), (rows, 1), 0, top)
    return jnp.take_along_axis(listing, (jnp.arange(top)[None, :] + turn) % top, axis=1)


def portions_of(number_of, total, bound, skew, full):
    portions = [(1 << 20) // math.isqrt(rank ** skew) + 1 for rank in range(1, number_of + 1)]
    largest = bound if full else min(bound, max(-(-total // number_of), total * portions[0] // sum(portions)))
    least = 1 if total - largest >= number_of - 1 else 0
    given, spare = [largest] + [least] * (number_of - 1), total - largest - least * (number_of - 1)
    while spare > 0:
        candidates = [i for i in range(1, number_of) if given[i] < largest] or [i for i in range(1, number_of) if given[i] < bound]
        mass, remaining = sum([portions[i] for i in candidates]), spare
        for i in candidates:
            addition = min(bound - given[i], max(1, remaining * portions[i] // mass), spare)
            given[i] = given[i] + addition
            spare = spare - addition
    return np.array(given)


def scatter_about(rng, shape, scale, limit, cuts=(), held_as=jnp.bfloat16):
    values = jax.random.normal(rng, shape, jnp.float32) * scale
    if len(cuts) > 0:
        values = shard_levels(rng, shape, cuts, -0.22, 0.18) * values
    return jnp.clip(values, min=-limit, max=limit).astype(held_as)


def setup_inputs(seed: int = 0) -> dict:
    splits = jax.random.split(jax.random.key(seed), 6)
    hidden_in = scatter_about(splits[0], (EXPERTS, N_DP, ROWS, FF), 1.0, 6.0, ((0, 8), (1, 4)))
    down_weight = scatter_about(splits[1], (EXPERTS, FF, D), FF ** -0.5, 0.1875, ((0, 8),))
    routes_keys = jax.random.split(jax.random.fold_in(splits[2], 1), TOKENS // TOK_DEV)
    routes_turns = jax.random.permutation(jax.random.fold_in(splits[2], 3), TOKENS // TOK_DEV)
    routes = jax.vmap(lambda own, number: deal_out(jax.random.fold_in(splits[2], 2), own, number, TOK_DEV, EXPERTS, TOPK, CAP, 2))(routes_keys, routes_turns).reshape((TOKENS, TOPK))
    gate_prob = jnp.clip(jnp.exp(math.log(1.0) - 2.9957323 * jax.random.uniform(splits[3], (TOKENS, TOPK), jnp.float32) ** shard_levels(splits[3], (TOKENS, TOPK), ((0, 32),), -0.2, 0.2)), 0.05, 1.0)
    cotangent = scatter_about(splits[4], (TOKENS, D), 0.1, 0.59765625, ((0, 32),))
    return dict(hidden_in=hidden_in, down_weight=down_weight, routes=routes, gate_prob=gate_prob, cotangent=cotangent)


def slot_positions(routes):
    blocks = routes.reshape(-1, TOK_DEV * TOPK)
    onehot = (blocks[:, :, None] == jnp.arange(EXPERTS, dtype=jnp.int32)[None, None, :]).astype(jnp.int32)
    before = jnp.cumsum(onehot, axis=1) - onehot
    within = jnp.sum(before * onehot, axis=2)
    return within.reshape(-1).astype(jnp.int32)


def reference(hidden_in, down_weight, routes, gate_prob, cotangent):
    chosen = routes.reshape(-1).astype(jnp.int32)
    within = slot_positions(routes)
    pairs = jnp.arange(TOKENS * TOPK, dtype=jnp.int32)
    block = pairs // (TOK_DEV * TOPK)
    target = (chosen * N_DP + block // N_EXPERT) * ROWS + (block % N_EXPERT) * CAP + within
    table = jnp.full((EXPERTS * N_DP * ROWS,), TOKENS * TOPK, jnp.int32)
    table = table.at[target].set(pairs).reshape(EXPERTS, N_DP, ROWS)
    cot_padded = jnp.concatenate([cotangent.astype(jnp.float32), jnp.zeros((1, D), jnp.float32)], axis=0)
    prob_padded = jnp.concatenate([gate_prob.reshape(-1).astype(jnp.float32), jnp.zeros((1,), jnp.float32)], axis=0)

    def per_expert(carry, inputs):
        mixed_total, gate_total = carry
        rows_hidden, weight, pair_ids = inputs
        token_ids = pair_ids // TOPK
        weight_f = weight.astype(jnp.float32)
        rows_f = rows_hidden.astype(jnp.float32)
        produced = jnp.einsum("jrf,fd->jrd", rows_f, weight_f).astype(jnp.bfloat16)
        produced_f = produced.astype(jnp.float32)
        cot_rows = cot_padded[token_ids]
        prob_rows = prob_padded[pair_ids]
        slot_grads = (prob_rows[..., None] * cot_rows).astype(jnp.bfloat16)
        gate_terms = jnp.sum(cot_rows * produced_f, axis=-1)
        mixed_total = mixed_total.at[token_ids].add(prob_rows[..., None] * produced_f)
        gate_total = gate_total.at[pair_ids].set(gate_terms)
        slot_f = slot_grads.astype(jnp.float32)
        hidden_grad = jnp.einsum("jrd,fd->jrf", slot_f, weight_f).astype(jnp.bfloat16)
        partial_terms = jnp.einsum("jrf,jrd->jfd", rows_f, slot_f).astype(jnp.bfloat16)
        partial_terms = lax.optimization_barrier(partial_terms)
        weight_grad = jnp.sum(partial_terms.astype(jnp.float32), axis=0).astype(jnp.bfloat16)
        return (mixed_total, gate_total), (hidden_grad, weight_grad)

    start = (jnp.zeros((TOKENS + 1, D), jnp.float32), jnp.zeros((TOKENS * TOPK + 1,), jnp.float32))
    (mixed_total, gate_total), (hidden_grad, weight_grad) = lax.scan(per_expert, start, (hidden_in, down_weight, table))
    combined = mixed_total[:TOKENS].astype(jnp.bfloat16)
    gate_grad = gate_total[:TOKENS * TOPK].reshape(TOKENS, TOPK)
    return combined, gate_grad, hidden_grad, weight_grad
```

```python
import jax
import jax.numpy as jnp
from jax import lax
from jax.sharding import PartitionSpec as P

BF16 = jnp.bfloat16
F32 = jnp.float32
CHUNKS = 2


def split_expert(n):
    nx = 1
    while nx * nx * 4 <= n:
        nx *= 2
    while n % nx:
        nx -= 1
    return n // nx, nx


def dot(a, b):
    return jnp.dot(a, b, preferred_element_type=F32)


def build(n_dp, n_expert):
    nz, nx = split_expert(n_expert)
    nc = 2 if n_dp % 2 == 0 else 1
    ny = n_dp // nc

    def along_z(move):
        return [
            (z * nx + x, move(z) * nx + x)
            for z in range(nz)
            for x in range(nx)
            if move(z) is not None
        ]

    def shift_z(r):
        return along_z(lambda z: (z + r) % nz)

    def line(step, first, last):
        return along_z(lambda z: z + step if first <= z <= last and 0 <= z + step < nz else None)

    def shift_x(q):
        return [(z * nx + x, z * nx + (x + q) % nx) for z in range(nz) for x in range(nx)]

    def shift_y(o):
        return [(y * nc + c, (y + o) % ny * nc + c) for y in range(ny) for c in range(nc)]

    swap_core = [(y * nc + c, y * nc + (c + 1) % nc) for y in range(ny) for c in range(nc)]

    def over_expert(a, pairs):
        return lax.ppermute(a, "expert", pairs)

    def over_dp(a, pairs):
        return lax.ppermute(a, "dp", pairs)

    def local(hidden_in, down_weight, routes, gate_prob, cotangent):
        me = lax.axis_index("expert")
        z, x = me // nx, me % nx
        dp = lax.axis_index("dp")
        y, core = dp // nc, dp % nc
        cap = hidden_in.shape[2] // n_expert
        ff = hidden_in.shape[3]
        tok, top = routes.shape
        features = down_weight.shape[2]
        width = features // CHUNKS
        weight = down_weight[0]

        table = jnp.concatenate([routes.astype(F32), gate_prob], axis=1).T
        tables = jnp.stack([table] + [over_expert(table, shift_z(r)) for r in range(1, nz)])
        line_routes = tables[:, :top].astype(jnp.int32)
        line_gates = tables[:, top:]
        here = z * nx + (x + jnp.arange(nx, dtype=jnp.int32)) % nx

        def slots_of(routed, ids):
            named = routed[..., None, :, :] == ids[:, None, None]
            match = named.any(axis=-2)
            count = match.astype(jnp.int32)
            before = jnp.cumsum(count, axis=-1) - count
            slot = jnp.arange(cap, dtype=jnp.int32)[:, None]
            onehot = match[..., None, :] & (before[..., None, :] == slot)
            return onehot, named

        onehot, named = slots_of(line_routes, here)
        token_gate = jnp.sum(jnp.where(named, line_gates[:, None], 0.0), axis=-2)
        slot_gate = jnp.sum(jnp.where(onehot, token_gate[..., None, :], 0.0), axis=-1)
        pick = onehot.astype(BF16).reshape(nz, nx * cap, tok)
        spread = jnp.where(onehot, token_gate[..., None, :], 0.0).astype(BF16)
        spread = spread.reshape(nz, nx * cap, tok)
        slot_gate = slot_gate.reshape(nz, nx * cap, 1)

        blocks = hidden_in.reshape(nz, nx, cap, ff)
        order_z = (z - jnp.arange(nz)) % nz
        order_x = (x + jnp.arange(nx)) % nx
        hidden = blocks[order_z][:, order_x].transpose(1, 0, 2, 3).reshape(-1, ff)

        rows = ff // n_dp
        hidden_t = hidden.T.reshape(ny, nc, rows, -1)
        hidden_t = hidden_t[(y + 1 + jnp.arange(ny)) % ny][:, (core + 1 + jnp.arange(nc)) % nc]
        hidden_t = hidden_t.transpose(1, 0, 2, 3).reshape(nc, ny * rows, -1)

        line_rows = nz * cap

        def dispatch(cot):
            low, high = [cot], [cot]
            for k in range(1, nz):
                low.append(over_expert(low[-1], line(1, k - 1, nz - 2)))
                high.append(over_expert(high[-1], line(-1, 1, nz - k)))
            held = [cot] + [jnp.where(z >= r, low[r], high[nz - r]) for r in range(1, nz)]
            held = jnp.stack(held)
            packed = lax.dot_general(
                pick, held, (((2,), (1,)), ((0,), (0,))), preferred_element_type=F32
            )
            packed = (packed * slot_gate).astype(BF16).reshape(nz, nx, cap, -1)
            out = [packed[:, 0].reshape(line_rows, -1)]
            for q in range(1, nx):
                out.append(over_expert(packed[:, q].reshape(line_rows, -1), shift_x(q)))
            return [out[-q % nx] for q in range(nx)]

        def combine(weight_c):
            produced = dot(hidden, weight_c).astype(BF16).reshape(nx, line_rows, -1)
            got = [produced[0]]
            for q in range(1, nx):
                got.append(over_expert(produced[q], shift_x(q)))
            rows_in = jnp.stack([got[-q % nx].reshape(nz, cap, -1) for q in range(nx)], axis=1)
            rows_in = rows_in.reshape(nz, nx * cap, -1)
            part = lax.dot_general(
                spread, rows_in, (((1,), (1,)), ((0,), (0,))), preferred_element_type=F32
            ).astype(BF16)
            up, down = None, None
            for k in range(1, nz):
                mine = part[k] if up is None else part[k] + up
                up = over_expert(mine, line(1, 0, k - 1))
                mine = part[nz - k] if down is None else part[nz - k] + down
                down = over_expert(mine, line(-1, nz - k, nz - 1))
            total = part[0].astype(F32)
            for other in (up, down):
                if other is not None:
                    total = total + other.astype(F32)
            return total.astype(BF16)

        def weight_part(slot_rows):
            give = dot(hidden_t[0], slot_rows).astype(BF16)
            if nc == 2:
                got = over_dp(give, swap_core)
                keep = dot(hidden_t[1], slot_rows).astype(BF16)
                keep = (keep.astype(F32) + got.astype(F32)).astype(BF16)
            else:
                keep = give
            keep = keep.reshape(ny, rows, -1)
            total = keep[ny - 1].astype(F32)
            for o in range(1, ny):
                total = total + over_dp(keep[o - 1], shift_y(o)).astype(F32)
            return total.astype(BF16)

        combined, weight_grad, slot_grads = [], [], []
        for c in range(CHUNKS):
            columns = slice(c * width, (c + 1) * width)
            slot_rows = jnp.concatenate(dispatch(cotangent[:, columns]), axis=0)
            slot_grads.append(slot_rows)
            combined.append(combine(weight[:, columns]))
            weight_grad.append(weight_part(slot_rows))

        hidden_grad = 0.0
        for c in range(CHUNKS):
            columns = slice(c * width, (c + 1) * width)
            hidden_grad = hidden_grad + lax.dot_general(
                slot_grads[c], weight[:, columns], (((1,), (1,)), ((), ())),
                preferred_element_type=F32,
            )
        scalars = jnp.sum(hidden_grad * hidden.astype(F32), axis=1).reshape(nx, line_rows)
        out = hidden_grad.astype(BF16).reshape(nx, nz, cap, ff)
        out = out[(jnp.arange(nx) - x) % nx][:, (z - jnp.arange(nz)) % nz]
        out = out.transpose(1, 0, 2, 3).reshape(hidden_in.shape)

        back = [scalars[0]] + [over_expert(scalars[q], shift_x(q)) for q in range(1, nx)]
        back = jnp.stack(back).reshape(nx, nz, cap)
        home = [back[:, 0]] + [over_expert(back[:, r], shift_z(-r)) for r in range(1, nz)]
        home = jnp.stack(home).reshape(n_expert, cap)
        far_z = (z + jnp.arange(nz, dtype=jnp.int32)) % nz
        far_x = (x - jnp.arange(nx, dtype=jnp.int32)) % nx
        ids = (far_z[:, None] * nx + far_x[None, :]).reshape(-1)
        mine, said = slots_of(routes.T, ids)
        by_token = jnp.sum(jnp.where(mine, home[:, :, None], 0.0), axis=1)
        gate_grad = jnp.sum(jnp.where(said, by_token[:, None], 0.0), axis=0).T / gate_prob
        return (
            jnp.concatenate(combined, axis=1),
            gate_grad,
            out,
            jnp.concatenate(weight_grad, axis=1)[None],
        )

    return local


def solution(mesh):
    in_specs = (
        P("expert", "dp", None, None),
        P("expert", None, None),
        P(("dp", "expert"), None),
        P(("dp", "expert"), None),
        P(("dp", "expert"), None),
    )
    out_specs = (
        P(("dp", "expert"), None),
        P(("dp", "expert"), None),
        P("expert", "dp", None, None),
        P("expert", "dp", None),
    )
    local = build(mesh.shape["dp"], mesh.shape["expert"])
    return jax.shard_map(local, mesh=mesh, in_specs=in_specs, out_specs=out_specs, check_vma=False)
```

```python
import math

import jax
import jax.numpy as jnp
from jax import lax
from jax.experimental import pallas as pl
from jax.experimental.pallas import tpu as pltpu
from jax.sharding import PartitionSpec as P

BF16 = jnp.bfloat16
F32 = jnp.float32
CHUNKS = 2
COST = 10**11
COSTS = {'kept2': 1}
LIMIT = 24
LIMITS = {'hidden': 60, 'made': 60}


def split_expert(n):
    nx = 1
    while nx * nx * 4 <= n:
        nx *= 2
    while n % nx:
        nx -= 1
    return n // nx, nx


def dot(a, b):
    return jnp.dot(a, b, preferred_element_type=F32)


def build_line(n_dp, n_expert):
    nz, nx = split_expert(n_expert)
    nc = 2 if n_dp % 2 == 0 else 1
    ny = n_dp // nc

    def along_z(move):
        return [
            (z * nx + x, move(z) * nx + x)
            for z in range(nz)
            for x in range(nx)
            if move(z) is not None
        ]

    def shift_z(r):
        return along_z(lambda z: (z + r) % nz)

    def line(step, first, last):
        return along_z(lambda z: z + step if first <= z <= last and 0 <= z + step < nz else None)

    def shift_x(q):
        return [(z * nx + x, z * nx + (x + q) % nx) for z in range(nz) for x in range(nx)]

    def shift_y(o):
        return [(y * nc + c, (y + o) % ny * nc + c) for y in range(ny) for c in range(nc)]

    swap_core = [(y * nc + c, y * nc + (c + 1) % nc) for y in range(ny) for c in range(nc)]

    def over_expert(a, pairs):
        return lax.ppermute(a, "expert", pairs)

    def over_dp(a, pairs):
        return lax.ppermute(a, "dp", pairs)

    def local(hidden_in, down_weight, routes, gate_prob, cotangent):
        me = lax.axis_index("expert")
        z, x = me // nx, me % nx
        dp = lax.axis_index("dp")
        y, core = dp // nc, dp % nc
        cap = hidden_in.shape[2] // n_expert
        ff = hidden_in.shape[3]
        tok, top = routes.shape
        features = down_weight.shape[2]
        width = features // CHUNKS
        weight = down_weight[0]

        table = jnp.concatenate([routes.astype(F32), gate_prob], axis=1).T
        tables = jnp.stack([table] + [over_expert(table, shift_z(r)) for r in range(1, nz)])
        line_routes = tables[:, :top].astype(jnp.int32)
        line_gates = tables[:, top:]
        here = z * nx + (x + jnp.arange(nx, dtype=jnp.int32)) % nx

        def slots_of(routed, ids):
            named = routed[..., None, :, :] == ids[:, None, None]
            match = named.any(axis=-2)
            count = match.astype(jnp.int32)
            before = jnp.cumsum(count, axis=-1) - count
            slot = jnp.arange(cap, dtype=jnp.int32)[:, None]
            onehot = match[..., None, :] & (before[..., None, :] == slot)
            return onehot, named

        onehot, named = slots_of(line_routes, here)
        token_gate = jnp.sum(jnp.where(named, line_gates[:, None], 0.0), axis=-2)
        slot_gate = jnp.sum(jnp.where(onehot, token_gate[..., None, :], 0.0), axis=-1)
        pick = onehot.astype(BF16).reshape(nz, nx * cap, tok)
        spread = jnp.where(onehot, token_gate[..., None, :], 0.0).astype(BF16)
        spread = spread.reshape(nz, nx * cap, tok)
        slot_gate = slot_gate.reshape(nz, nx * cap, 1)

        blocks = hidden_in.reshape(nz, nx, cap, ff)
        order_z = (z - jnp.arange(nz)) % nz
        order_x = (x + jnp.arange(nx)) % nx
        hidden = blocks[order_z][:, order_x].transpose(1, 0, 2, 3).reshape(-1, ff)

        rows = ff // n_dp
        hidden_t = hidden.T.reshape(ny, nc, rows, -1)
        hidden_t = hidden_t[(y + 1 + jnp.arange(ny)) % ny][:, (core + 1 + jnp.arange(nc)) % nc]
        hidden_t = hidden_t.transpose(1, 0, 2, 3).reshape(nc, ny * rows, -1)

        line_rows = nz * cap

        def dispatch(cot):
            low, high = [cot], [cot]
            for k in range(1, nz):
                low.append(over_expert(low[-1], line(1, k - 1, nz - 2)))
                high.append(over_expert(high[-1], line(-1, 1, nz - k)))
            held = [cot] + [jnp.where(z >= r, low[r], high[nz - r]) for r in range(1, nz)]
            held = jnp.stack(held)
            packed = lax.dot_general(
                pick, held, (((2,), (1,)), ((0,), (0,))), preferred_element_type=F32
            )
            packed = (packed * slot_gate).astype(BF16).reshape(nz, nx, cap, -1)
            out = [packed[:, 0].reshape(line_rows, -1)]
            for q in range(1, nx):
                out.append(over_expert(packed[:, q].reshape(line_rows, -1), shift_x(q)))
            return [out[-q % nx] for q in range(nx)]

        def combine(weight_c):
            produced = dot(hidden, weight_c).astype(BF16).reshape(nx, line_rows, -1)
            got = [produced[0]]
            for q in range(1, nx):
                got.append(over_expert(produced[q], shift_x(q)))
            rows_in = jnp.stack([got[-q % nx].reshape(nz, cap, -1) for q in range(nx)], axis=1)
            rows_in = rows_in.reshape(nz, nx * cap, -1)
            part = lax.dot_general(
                spread, rows_in, (((1,), (1,)), ((0,), (0,))), preferred_element_type=F32
            ).astype(BF16)
            up, down = None, None
            for k in range(1, nz):
                mine = part[k] if up is None else part[k] + up
                up = over_expert(mine, line(1, 0, k - 1))
                mine = part[nz - k] if down is None else part[nz - k] + down
                down = over_expert(mine, line(-1, nz - k, nz - 1))
            total = part[0].astype(F32)
            for other in (up, down):
                if other is not None:
                    total = total + other.astype(F32)
            return total.astype(BF16)

        def weight_part(slot_rows):
            give = dot(hidden_t[0], slot_rows).astype(BF16)
            if nc == 2:
                got = over_dp(give, swap_core)
                keep = dot(hidden_t[1], slot_rows).astype(BF16)
                keep = (keep.astype(F32) + got.astype(F32)).astype(BF16)
            else:
                keep = give
            keep = keep.reshape(ny, rows, -1)
            total = keep[ny - 1].astype(F32)
            for o in range(1, ny):
                total = total + over_dp(keep[o - 1], shift_y(o)).astype(F32)
            return total.astype(BF16)

        combined, weight_grad, slot_grads = [], [], []
        for c in range(CHUNKS):
            columns = slice(c * width, (c + 1) * width)
            slot_rows = jnp.concatenate(dispatch(cotangent[:, columns]), axis=0)
            slot_grads.append(slot_rows)
            combined.append(combine(weight[:, columns]))
            weight_grad.append(weight_part(slot_rows))

        hidden_grad = 0.0
        for c in range(CHUNKS):
            columns = slice(c * width, (c + 1) * width)
            hidden_grad = hidden_grad + lax.dot_general(
                slot_grads[c], weight[:, columns], (((1,), (1,)), ((), ())),
                preferred_element_type=F32,
            )
        scalars = jnp.sum(hidden_grad * hidden.astype(F32), axis=1).reshape(nx, line_rows)
        out = hidden_grad.astype(BF16).reshape(nx, nz, cap, ff)
        out = out[(jnp.arange(nx) - x) % nx][:, (z - jnp.arange(nz)) % nz]
        out = out.transpose(1, 0, 2, 3).reshape(hidden_in.shape)

        back = [scalars[0]] + [over_expert(scalars[q], shift_x(q)) for q in range(1, nx)]
        back = jnp.stack(back).reshape(nx, nz, cap)
        home = [back[:, 0]] + [over_expert(back[:, r], shift_z(-r)) for r in range(1, nz)]
        home = jnp.stack(home).reshape(n_expert, cap)
        far_z = (z + jnp.arange(nz, dtype=jnp.int32)) % nz
        far_x = (x - jnp.arange(nx, dtype=jnp.int32)) % nx
        ids = (far_z[:, None] * nx + far_x[None, :]).reshape(-1)
        mine, said = slots_of(routes.T, ids)
        by_token = jnp.sum(jnp.where(mine, home[:, :, None], 0.0), axis=1)
        gate_grad = jnp.sum(jnp.where(said, by_token[:, None], 0.0), axis=0).T / gate_prob
        return (
            jnp.concatenate(combined, axis=1),
            gate_grad,
            out,
            jnp.concatenate(weight_grad, axis=1)[None],
        )

    return local


def nothing(*refs):
    pass


def after(x, *deps):
    anywhere = pl.BlockSpec(memory_space=pl.ANY)
    return pl.pallas_call(
        nothing,
        out_shape=jax.ShapeDtypeStruct(x.shape, x.dtype),
        in_specs=[anywhere] * (1 + len(deps)),
        out_specs=anywhere,
        input_output_aliases={0: 0},
        name="after",
    )(x, *deps)


def call(kernel, grid, ins, outs, scratch, scalars, deps, cost):
    n_in, n_dep = len(ins), len(deps)
    n_scalar = 0 if scalars is None else 1

    def body(*refs):
        first = n_scalar + n_in
        kernel(*refs[:first], *refs[first + n_dep:])

    specs = [pl.BlockSpec(block, index) for _, block, index in ins]
    specs += [pl.BlockSpec(memory_space=pl.ANY)] * n_dep
    return pl.pallas_call(
        body,
        out_shape=[jax.ShapeDtypeStruct(shape, dtype) for shape, dtype, _, _ in outs],
        grid_spec=pltpu.PrefetchScalarGridSpec(
            num_scalar_prefetch=n_scalar,
            grid=grid,
            in_specs=specs,
            out_specs=[pl.BlockSpec(block, index) for _, _, block, index in outs],
            scratch_shapes=list(scratch),
        ),
        compiler_params=pltpu.CompilerParams(vmem_limit_bytes=LIMITS.get(kernel.__name__, LIMIT) << 20),
        cost_estimate=pl.CostEstimate(flops=cost, bytes_accessed=cost // 300, transcendentals=0),
        name=kernel.__name__,
    )(*([] if scalars is None else [scalars]), *[a for a, _, _ in ins], *deps)


def build_tree(n_dp, n_expert):
    nz, nx, nc, ny = 4, 2, 2, 2

    def along_z(pairs):
        return [(a * nx + x, b * nx + x) for a, b in pairs for x in range(nx)]

    buddy = along_z([(0, 1), (1, 0), (2, 3), (3, 2)])
    middle = along_z([(1, 2), (2, 1)])
    skip = along_z([(0, 2), (2, 0), (1, 3), (3, 1)])
    mirror = along_z([(0, 3), (3, 0), (1, 2), (2, 1)])
    inward = along_z([(0, 1), (3, 2)])
    outward = along_z([(1, 0), (2, 3)])
    swap_x = [(e, e ^ 1) for e in range(n_expert)]
    swap_core = [(d, d ^ 1) for d in range(n_dp)]
    swap_y = [(d, d ^ 2) for d in range(n_dp)]

    def over_expert(a, pairs):
        return lax.ppermute(a, "expert", pairs)

    def over_dp(a, pairs):
        return lax.ppermute(a, "dp", pairs)

    def local(hidden_in, down_weight, routes, gate_prob, cotangent):
        me = lax.axis_index("expert")
        z, x = me // nx, me % nx
        dp = lax.axis_index("dp")
        cap = hidden_in.shape[2] // n_expert
        ff = hidden_in.shape[3]
        tok, top = routes.shape
        features = down_weight.shape[2]
        tile = 512
        tiles = features // tile
        first = tiles // 2
        begin, count = (0, first), (first, tiles - first)
        widths = [n * tile for n in count]
        spans = [(b * tile, (b + n) * tile) for b, n in zip(begin, count)]
        half = 2 * cap
        part = ff // n_dp
        last, named = [], []

        def chain(kernel, grid, ins, outs, scratch=(), deps=(), flops=0):
            named.append(kernel.__name__)
            cost = COSTS.get(f"{named[-1]}{named.count(named[-1])}", COST)
            got = call(kernel, grid, ins, outs, scratch, scalars, tuple(last) + tuple(deps), cost)
            last[:] = [got[0]]
            return got

        def hold(a, *deps):
            a = after(a, *last, *deps)
            last[:] = [a]
            return a
        blocks_in = hidden_in.reshape(n_expert, cap, ff)
        is_middle = (z == 1) | (z == 2)
        low = z < 2
        order_z = jnp.stack([z, z ^ 1, jnp.where(low, 2, 1), jnp.where(low, 3, 0)])
        order_x = jnp.stack([x, x ^ 1])
        order = (order_z[None, :] * nx + order_x[:, None]).reshape(-1)
        parts = jnp.stack([dp ^ 3, dp ^ 1, dp ^ 2, dp])
        scalars = jnp.concatenate(
            [order, parts, jnp.stack([is_middle.astype(jnp.int32), z * nx + x, z * nx + (x ^ 1)])]
        ).astype(jnp.int32)
        at_parts, at_middle, at_here = n_expert, n_expert + n_dp, n_expert + n_dp + 1

        buddies = over_expert(cotangent, buddy)
        mids = over_expert(cotangent, middle)
        table = jnp.concatenate([routes.astype(F32), gate_prob], axis=1).T
        pair = jnp.concatenate([table, over_expert(table, buddy)])
        far_pair = over_expert(pair, skip)

        def whole(a):
            return (a, a.shape, lambda *_: (0,) * a.ndim)

        def sliced(body, fixed):
            def run(s, *refs):
                kept, moving = refs[:fixed], refs[fixed:]
                for k in range(moving[-1].shape[-1] // tile):
                    body(s, *kept, *(ref.at[:, k * tile:(k + 1) * tile] for ref in moving))

            run.__name__ = body.__name__
            return run

        def strip_of(a):
            return (a, a.shape, lambda *_: (0, 0))

        def strip_out(rows, c, dtype=BF16):
            return ((rows, widths[c]), dtype, (rows, widths[c]), lambda *_: (0, 0))

        def columns(a, first=0):
            return (a, (a.shape[0], tile), lambda j, *_: (0, first + j))

        def wide(rows, c, dtype=BF16):
            return ((rows, widths[c]), dtype, (rows, tile), lambda j, *_: (0, j))

        def full(rows, dtype=BF16):
            return ((rows, features), dtype, (rows, tile), lambda j, *_: (0, j))

        broad = features // 4

        def broadly(rows):
            return ((rows, features), BF16, (rows, broad), lambda j, *_: (0, j))

        def product(q):
            def made(s, *refs):
                *given, w, near_ref, far_ref, last_ref, rows = refs

                @pl.when(pl.program_id(0) == 0)
                def _():
                    for i, ref in enumerate(given):
                        rows[i * cap:(i + 1) * cap] = ref[0]

                out = dot(rows[...], w[0]).astype(BF16)
                near_ref[...] = out[:half]
                far_ref[...] = out[half:half + cap]
                last_ref[...] = out[half + cap:]

            ins = [
                (blocks_in, (1, cap, ff), lambda j, s, i=i: (s[q * nz + i], 0, 0)) for i in range(nz)
            ]
            ins.append((down_weight, (1, ff, broad), lambda j, s: (0, 0, j)))
            return chain(
                made, (features // broad,), ins, [broadly(half), broadly(cap), broadly(cap)],
                [pltpu.VMEM((nz * cap, ff), BF16)],
            )

        there_near, there_far, there_last = product(1)
        rs_last = over_expert(there_last, swap_x)
        rs_far = over_expert(there_far, swap_x)
        rs_near = over_expert(there_near, swap_x)

        here_near, here_far, here_last = product(0)

        def onehot(pos_ref, row):
            slot = lax.broadcasted_iota(jnp.int32, (cap, tok), 0)
            return slot == pos_ref[row:row + 1, :]

        def pack_rows(pos_ref, gate_ref, first, held, send_ref, keep_ref):
            for i, block in enumerate(held):
                for q, ref in enumerate((keep_ref, send_ref)):
                    row = (first + i) * nx + q
                    hot = onehot(pos_ref, row)
                    scale = jnp.sum(
                        jnp.where(hot, gate_ref[row:row + 1, :], 0.0), axis=1, keepdims=True
                    )
                    rows = dot(hot.astype(BF16), block)
                    ref[i * cap:(i + 1) * cap] = (rows * scale).astype(BF16)

        def spread_rows(pos_ref, gate_ref, row, here, there):
            total = None
            for q, rows in enumerate((here, there)):
                at = row * nx + q
                weighted = jnp.where(onehot(pos_ref, at), gate_ref[at:at + 1, :], 0.0).astype(BF16)
                term = lax.dot_general(
                    weighted, rows, (((0,), (0,)), ((), ())), preferred_element_type=F32
                )
                total = term if total is None else total + term
            return total

        def entire(rows, dtype=BF16, cols=None):
            shape = (rows, features if cols is None else cols)
            return (shape, dtype, shape, lambda *_: (0, 0))

        def packed_near(s, pos_ref, gate_ref, own, other, send_ref, keep_ref):
            pack_rows(pos_ref, gate_ref, 0, (own[...], other[...]), send_ref, keep_ref)

        def packed_far(s, pos_ref, gate_ref, m0, o0, m1, o1, first_ref, second_ref, keep_ref):
            middle_here = s[at_middle] == 1
            for k in range(tiles):
                at = slice(k * tile, (k + 1) * tile)
                held = [
                    jnp.where(middle_here, a[:, at], b[:, at]) for a, b in ((m0, o0), (m1, o1))
                ]
                send, moved = (first_ref, 0) if k < first else (second_ref, first)
                send = send.at[:, (k - moved) * tile:(k - moved + 1) * tile]
                pack_rows(pos_ref, gate_ref, 2, held, send, keep_ref.at[:, at])

        def shared_far(s, pos_ref, gate_ref, here2, there2, here3, there3, far_ref, last_ref):
            for row, here, there, ref in ((2, here2, there2, far_ref), (3, here3, there3, last_ref)):
                total = spread_rows(pos_ref, gate_ref, row, here[...], there[...])
                ref[...] = total.astype(BF16)

        def shared_near(s, pos_ref, gate_ref, here, there, sum_ref, keep_ref, send_ref):
            for i, ref in enumerate((keep_ref, send_ref)):
                lines = slice(i * cap, (i + 1) * cap)
                total = spread_rows(pos_ref, gate_ref, i, here[lines], there[lines])
                if i == 1:
                    total = total + sum_ref[...].astype(F32)
                ref[...] = total.astype(ref.dtype)

        def plus(a, b):
            def add(s, a_ref, b_ref, out_ref):
                out_ref[...] = a_ref[...] + b_ref[...]

            return chain(add, (1,), [whole(a), whole(b)], [entire(tok)])[0]

        def turned(s, *refs):
            *given, out_ref, rows = refs

            @pl.when(pl.program_id(0) == 0)
            def _():
                for i, ref in enumerate(given):
                    rows[i * cap:(i + 1) * cap] = ref[0]

            first = pl.multiple_of(s[at_parts + pl.program_id(0)] * part, part)
            out_ref[...] = rows[:, pl.ds(first, part)].T

        slots = n_expert * cap
        (hidden_t,) = chain(
            turned, (n_dp,),
            [(blocks_in, (1, cap, ff), lambda j, s, i=i: (s[i], 0, 0)) for i in range(n_expert)],
            [((ff, slots), BF16, (part, slots), lambda j, *_: (j, 0))],
            [pltpu.VMEM((slots, ff), BF16)],
        )

        def positions(s, near_ref, far_ref, pos_ref, gate_ref):
            middle_here = s[at_middle] == 1
            rows = 2 * top
            held = [
                near_ref[:rows],
                near_ref[rows:],
                jnp.where(middle_here, far_ref[rows:], far_ref[:rows]),
                jnp.where(middle_here, far_ref[:rows], far_ref[rows:]),
            ]
            match, gates = [], []
            for t in held:
                for q in range(nx):
                    named = t[:top] == s[at_here + q].astype(F32)
                    match.append(jnp.sum(named.astype(F32), axis=0, keepdims=True))
                    gates.append(jnp.sum(jnp.where(named, t[top:], 0.0), axis=0, keepdims=True))
            match = jnp.concatenate(match, axis=0)
            earlier = lax.broadcasted_iota(jnp.int32, (tok, tok), 0) < lax.broadcasted_iota(
                jnp.int32, (tok, tok), 1
            )
            before = dot(match.astype(BF16), earlier.astype(BF16))
            pos_ref[...] = jnp.where(match > 0, before, -1.0).astype(jnp.int32)
            gate_ref[...] = jnp.concatenate(gates, axis=0)

        small = (nz * nx, tok)
        pos, gate = chain(
            positions, (1,), [whole(pair), whole(far_pair)],
            [(small, jnp.int32, small, lambda *_: (0, 0)), (small, F32, small, lambda *_: (0, 0))],
        )
        def pieces(c):
            whole_width = [columns(a, begin[c]) for a in (own_near, own_far, ag_near)]
            return whole_width + [columns(ag_far[c])]

        share_rows = ny * part

        def stack_pieces(given, rows):
            for i, ref in enumerate(given):
                rows[i * half:(i + 1) * half] = ref[...]

        def weight_give(c):
            def gave(s, *refs):
                *given, turned_ref, out_ref, rows_ref = refs
                stack_pieces(given, rows_ref)
                out_ref[...] = dot(turned_ref[...], rows_ref[...]).astype(BF16)

            return chain(
                gave, (count[c],),
                pieces(c) + [(hidden_t, (share_rows, slots), lambda *_: (0, 0))],
                [wide(share_rows, c), wide(slots, c)],
            )

        def weight_keep(rows, c, got):
            def kept(s, rows_ref, turned_ref, got_ref, send_ref, keep_ref):
                out = dot(turned_ref[...], rows_ref[...]).astype(BF16).astype(F32)
                out = out + got_ref[...].astype(F32)
                send_ref[...] = out[:part].astype(BF16)
                keep_ref[...] = out[part:]

            return chain(
                kept, (count[c],),
                [columns(rows), (hidden_t, (share_rows, slots), lambda *_: (1, 0)), columns(got)],
                [wide(part, c), wide(part, c, F32)],
            )

        def hidden_all(rows_a, rows_b, deps):
            strip = 256

            def hidden(s, a_ref, b_ref, w, h, out_ref, scalar_ref):
                j = pl.program_id(0)
                total = None
                for ref, (first, end) in zip((a_ref, b_ref), spans):
                    term = lax.dot_general(
                        ref[...], w[0, :, first:end], (((1,), (1,)), ((), ())),
                        preferred_element_type=F32,
                    )
                    total = term if total is None else total + term
                for i in range(n_expert):
                    mine = total[i * cap:(i + 1) * cap]
                    out_ref[s[i]] = mine.astype(BF16)
                    term = jnp.sum(mine * h[s[i]].astype(F32), axis=1, keepdims=True)
                    term = jnp.broadcast_to(term, (cap, 128))

                    @pl.when(j == 0)
                    def _():
                        scalar_ref[i] = term

                    @pl.when(j > 0)
                    def _():
                        scalar_ref[i] += term

            strips = (n_expert, cap, strip)
            return chain(
                hidden, (ff // strip,),
                [
                    whole(rows_a), whole(rows_b),
                    (down_weight, (1, strip, features), lambda j, s: (0, j, 0)),
                    (blocks_in, strips, lambda j, s: (0, 0, j)),
                ],
                [
                    (blocks_in.shape, BF16, strips, lambda j, s: (0, 0, j)),
                    ((n_expert, cap, 128), F32, (n_expert, cap, 128), lambda *_: (0, 0, 0)),
                ],
                (), deps,
            )

        mids = hold(mids, buddies)
        mid_last = over_expert(buddies, middle)
        out_far = over_expert(mids, outward)
        send, own_near = chain(
            sliced(packed_near, 2), (1,),
            [whole(a) for a in (pos, gate, cotangent, buddies)], [entire(half), entire(half)],
        )
        ag_near = over_expert(send, swap_x)
        sum_far, sum_last = chain(
            sliced(shared_far, 2), (1,),
            [whole(a) for a in (pos, gate, here_far, rs_far, here_last, rs_last)],
            [entire(tok), entire(tok)],
        )
        one = over_expert(sum_last, inward)
        mid_last = hold(mid_last, out_far)
        out_last = over_expert(mid_last, outward)
        two = over_expert(plus(sum_last, one), middle)
        sum_far = hold(sum_far, one)
        one_far = over_expert(sum_far, inward)
        send_a, send_b, own_far = chain(
            packed_far, (1,),
            [whole(a) for a in (pos, gate, mids, out_far, mid_last, out_last)],
            [entire(half, BF16, widths[0]), entire(half, BF16, widths[1]), entire(half)],
        )
        ag_far = [over_expert(send_a, swap_x), over_expert(send_b, swap_x)]
        two_far = over_expert(plus(sum_far, one_far), middle)
        give, rows_a = weight_give(0)
        got = over_dp(give, swap_core)
        keep, give = chain(
            sliced(shared_near, 2), (1,),
            [whole(a) for a in (pos, gate, here_near, rs_near, two)],
            [entire(tok, F32), entire(tok)],
        )
        three = over_expert(give, buddy)
        send_a, keep_a = weight_keep(rows_a, 0, got)
        got_a = over_dp(send_a, swap_y)
        give, rows_b = weight_give(1)
        got = over_dp(give, swap_core)
        hidden_grad, scalar_rows = hidden_all(rows_a, rows_b, ())
        two_far = hold(two_far)
        send_b, keep_b = weight_keep(rows_b, 1, got)
        got_b = over_dp(send_b, swap_y)
        scalar_rows = hold(scalar_rows)
        three = hold(three)
        got_a = hold(got_a)

        def add_three(s, a, b, c, out_ref):
            total = a[...] + b[...].astype(F32) + c[...].astype(F32)
            out_ref[...] = total.astype(BF16)

        (combined,) = chain(
            add_three, (1,), [whole(a) for a in (keep, three, two_far)], [entire(tok)]
        )

        def add_chunks(s, *refs):
            *given, out_ref = refs
            for c in range(2):
                total = given[2 * c][...] + given[2 * c + 1][...].astype(F32)
                out_ref[0, :, spans[c][0]:spans[c][1]] = total.astype(BF16)

        strip = part // 2
        (weight_grad,) = chain(
            add_chunks, (2,),
            [(a, (strip, a.shape[1]), lambda j, *_: (j, 0)) for a in (keep_a, got_a, keep_b, got_b)],
            [((1, part, features), BF16, (1, strip, features), lambda j, *_: (0, j, 0))],
        )

        back = scalar_rows[:, :, 0].reshape(nx, nz, cap)
        back = jnp.stack([back[0], over_expert(back[1], swap_x)], axis=1)
        home = jnp.stack(
            [
                back[0],
                over_expert(back[1], buddy),
                over_expert(jnp.where(is_middle, back[3], back[2]), skip),
                over_expert(jnp.where(is_middle, back[2], back[3]), mirror),
            ]
        ).reshape(n_expert, cap)
        from_z = jnp.stack([z, z ^ 1, z ^ 2, 3 - z])
        ids = (from_z[:, None] * nx + order_x[None, :]).reshape(-1)
        said = routes.T[None] == ids[:, None, None]
        match = said.any(axis=1)
        count = match.astype(jnp.int32)
        before = jnp.cumsum(count, axis=1) - count
        slot = jnp.arange(cap, dtype=jnp.int32)[:, None]
        mine = match[:, None, :] & (before[:, None, :] == slot)
        by_token = jnp.sum(jnp.where(mine, home[:, :, None], 0.0), axis=1)
        gate_grad = jnp.sum(jnp.where(said, by_token[:, None], 0.0), axis=0).T / gate_prob
        return (
            combined,
            gate_grad,
            hidden_grad.reshape(hidden_in.shape),
            weight_grad,
        )

    return local


def build(n_dp, n_expert):
    if split_expert(n_expert) == (4, 2) and n_dp == 4:
        return build_tree(n_dp, n_expert)
    return build_line(n_dp, n_expert)


def solution(mesh):
    in_specs = (
        P("expert", "dp", None, None),
        P("expert", None, None),
        P(("dp", "expert"), None),
        P(("dp", "expert"), None),
        P(("dp", "expert"), None),
    )
    out_specs = (
        P(("dp", "expert"), None),
        P(("dp", "expert"), None),
        P("expert", "dp", None, None),
        P("expert", "dp", None),
    )
    local = build(mesh.shape["dp"], mesh.shape["expert"])
    return jax.shard_map(local, mesh=mesh, in_specs=in_specs, out_specs=out_specs, check_vma=False)
```

```python
import math

import jax
import jax.numpy as jnp
from jax import lax
from jax.experimental import pallas as pl
from jax.experimental.pallas import tpu as pltpu
from jax.sharding import PartitionSpec as P

BF16 = jnp.bfloat16
F32 = jnp.float32
CHUNKS = 2
COST = 10**11
COSTS = {'positions1': 1, 'packed_near1': 1, 'turned1': 1, 'kept2': 1}
LIMIT = 24
LIMITS = {'hidden': 60, 'made': 60}


def split_expert(n):
    nx = 1
    while nx * nx * 4 <= n:
        nx *= 2
    while n % nx:
        nx -= 1
    return n // nx, nx


def dot(a, b):
    return jnp.dot(a, b, preferred_element_type=F32)


def build_line(n_dp, n_expert):
    nz, nx = split_expert(n_expert)
    nc = 2 if n_dp % 2 == 0 else 1
    ny = n_dp // nc

    def along_z(move):
        return [
            (z * nx + x, move(z) * nx + x)
            for z in range(nz)
            for x in range(nx)
            if move(z) is not None
        ]

    def shift_z(r):
        return along_z(lambda z: (z + r) % nz)

    def line(step, first, last):
        return along_z(lambda z: z + step if first <= z <= last and 0 <= z + step < nz else None)

    def shift_x(q):
        return [(z * nx + x, z * nx + (x + q) % nx) for z in range(nz) for x in range(nx)]

    def shift_y(o):
        return [(y * nc + c, (y + o) % ny * nc + c) for y in range(ny) for c in range(nc)]

    swap_core = [(y * nc + c, y * nc + (c + 1) % nc) for y in range(ny) for c in range(nc)]

    def over_expert(a, pairs):
        return lax.ppermute(a, "expert", pairs)

    def over_dp(a, pairs):
        return lax.ppermute(a, "dp", pairs)

    def local(hidden_in, down_weight, routes, gate_prob, cotangent):
        me = lax.axis_index("expert")
        z, x = me // nx, me % nx
        dp = lax.axis_index("dp")
        y, core = dp // nc, dp % nc
        cap = hidden_in.shape[2] // n_expert
        ff = hidden_in.shape[3]
        tok, top = routes.shape
        features = down_weight.shape[2]
        width = features // CHUNKS
        weight = down_weight[0]

        table = jnp.concatenate([routes.astype(F32), gate_prob], axis=1).T
        tables = jnp.stack([table] + [over_expert(table, shift_z(r)) for r in range(1, nz)])
        line_routes = tables[:, :top].astype(jnp.int32)
        line_gates = tables[:, top:]
        here = z * nx + (x + jnp.arange(nx, dtype=jnp.int32)) % nx

        def slots_of(routed, ids):
            named = routed[..., None, :, :] == ids[:, None, None]
            match = named.any(axis=-2)
            count = match.astype(jnp.int32)
            before = jnp.cumsum(count, axis=-1) - count
            slot = jnp.arange(cap, dtype=jnp.int32)[:, None]
            onehot = match[..., None, :] & (before[..., None, :] == slot)
            return onehot, named

        onehot, named = slots_of(line_routes, here)
        token_gate = jnp.sum(jnp.where(named, line_gates[:, None], 0.0), axis=-2)
        slot_gate = jnp.sum(jnp.where(onehot, token_gate[..., None, :], 0.0), axis=-1)
        pick = onehot.astype(BF16).reshape(nz, nx * cap, tok)
        spread = jnp.where(onehot, token_gate[..., None, :], 0.0).astype(BF16)
        spread = spread.reshape(nz, nx * cap, tok)
        slot_gate = slot_gate.reshape(nz, nx * cap, 1)

        blocks = hidden_in.reshape(nz, nx, cap, ff)
        order_z = (z - jnp.arange(nz)) % nz
        order_x = (x + jnp.arange(nx)) % nx
        hidden = blocks[order_z][:, order_x].transpose(1, 0, 2, 3).reshape(-1, ff)

        rows = ff // n_dp
        hidden_t = hidden.T.reshape(ny, nc, rows, -1)
        hidden_t = hidden_t[(y + 1 + jnp.arange(ny)) % ny][:, (core + 1 + jnp.arange(nc)) % nc]
        hidden_t = hidden_t.transpose(1, 0, 2, 3).reshape(nc, ny * rows, -1)

        line_rows = nz * cap

        def dispatch(cot):
            low, high = [cot], [cot]
            for k in range(1, nz):
                low.append(over_expert(low[-1], line(1, k - 1, nz - 2)))
                high.append(over_expert(high[-1], line(-1, 1, nz - k)))
            held = [cot] + [jnp.where(z >= r, low[r], high[nz - r]) for r in range(1, nz)]
            held = jnp.stack(held)
            packed = lax.dot_general(
                pick, held, (((2,), (1,)), ((0,), (0,))), preferred_element_type=F32
            )
            packed = (packed * slot_gate).astype(BF16).reshape(nz, nx, cap, -1)
            out = [packed[:, 0].reshape(line_rows, -1)]
            for q in range(1, nx):
                out.append(over_expert(packed[:, q].reshape(line_rows, -1), shift_x(q)))
            return [out[-q % nx] for q in range(nx)]

        def combine(weight_c):
            produced = dot(hidden, weight_c).astype(BF16).reshape(nx, line_rows, -1)
            got = [produced[0]]
            for q in range(1, nx):
                got.append(over_expert(produced[q], shift_x(q)))
            rows_in = jnp.stack([got[-q % nx].reshape(nz, cap, -1) for q in range(nx)], axis=1)
            rows_in = rows_in.reshape(nz, nx * cap, -1)
            part = lax.dot_general(
                spread, rows_in, (((1,), (1,)), ((0,), (0,))), preferred_element_type=F32
            ).astype(BF16)
            up, down = None, None
            for k in range(1, nz):
                mine = part[k] if up is None else part[k] + up
                up = over_expert(mine, line(1, 0, k - 1))
                mine = part[nz - k] if down is None else part[nz - k] + down
                down = over_expert(mine, line(-1, nz - k, nz - 1))
            total = part[0].astype(F32)
            for other in (up, down):
                if other is not None:
                    total = total + other.astype(F32)
            return total.astype(BF16)

        def weight_part(slot_rows):
            give = dot(hidden_t[0], slot_rows).astype(BF16)
            if nc == 2:
                got = over_dp(give, swap_core)
                keep = dot(hidden_t[1], slot_rows).astype(BF16)
                keep = (keep.astype(F32) + got.astype(F32)).astype(BF16)
            else:
                keep = give
            keep = keep.reshape(ny, rows, -1)
            total = keep[ny - 1].astype(F32)
            for o in range(1, ny):
                total = total + over_dp(keep[o - 1], shift_y(o)).astype(F32)
            return total.astype(BF16)

        combined, weight_grad, slot_grads = [], [], []
        for c in range(CHUNKS):
            columns = slice(c * width, (c + 1) * width)
            slot_rows = jnp.concatenate(dispatch(cotangent[:, columns]), axis=0)
            slot_grads.append(slot_rows)
            combined.append(combine(weight[:, columns]))
            weight_grad.append(weight_part(slot_rows))

        hidden_grad = 0.0
        for c in range(CHUNKS):
            columns = slice(c * width, (c + 1) * width)
            hidden_grad = hidden_grad + lax.dot_general(
                slot_grads[c], weight[:, columns], (((1,), (1,)), ((), ())),
                preferred_element_type=F32,
            )
        scalars = jnp.sum(hidden_grad * hidden.astype(F32), axis=1).reshape(nx, line_rows)
        out = hidden_grad.astype(BF16).reshape(nx, nz, cap, ff)
        out = out[(jnp.arange(nx) - x) % nx][:, (z - jnp.arange(nz)) % nz]
        out = out.transpose(1, 0, 2, 3).reshape(hidden_in.shape)

        back = [scalars[0]] + [over_expert(scalars[q], shift_x(q)) for q in range(1, nx)]
        back = jnp.stack(back).reshape(nx, nz, cap)
        home = [back[:, 0]] + [over_expert(back[:, r], shift_z(-r)) for r in range(1, nz)]
        home = jnp.stack(home).reshape(n_expert, cap)
        far_z = (z + jnp.arange(nz, dtype=jnp.int32)) % nz
        far_x = (x - jnp.arange(nx, dtype=jnp.int32)) % nx
        ids = (far_z[:, None] * nx + far_x[None, :]).reshape(-1)
        mine, said = slots_of(routes.T, ids)
        by_token = jnp.sum(jnp.where(mine, home[:, :, None], 0.0), axis=1)
        gate_grad = jnp.sum(jnp.where(said, by_token[:, None], 0.0), axis=0).T / gate_prob
        return (
            jnp.concatenate(combined, axis=1),
            gate_grad,
            out,
            jnp.concatenate(weight_grad, axis=1)[None],
        )

    return local


def nothing(*refs):
    pass


def after(x, *deps):
    anywhere = pl.BlockSpec(memory_space=pl.ANY)
    return pl.pallas_call(
        nothing,
        out_shape=jax.ShapeDtypeStruct(x.shape, x.dtype),
        in_specs=[anywhere] * (1 + len(deps)),
        out_specs=anywhere,
        input_output_aliases={0: 0},
        name="after",
    )(x, *deps)


def call(kernel, grid, ins, outs, scratch, scalars, deps, cost):
    n_in, n_dep = len(ins), len(deps)
    n_scalar = 0 if scalars is None else 1

    def body(*refs):
        first, end = n_scalar + n_in, n_scalar + n_in + n_dep + len(outs) - 1
        refs[end][...] = jnp.zeros((8, 128), F32)
        kernel(*refs[:first], *refs[first + n_dep:end], *refs[end + 1:])

    outs = list(outs) + [((8, 128), F32, (8, 128), lambda *_: (0, 0))]

    specs = [pl.BlockSpec(block, index) for _, block, index in ins]
    specs += [pl.BlockSpec(memory_space=pl.ANY)] * n_dep
    return pl.pallas_call(
        body,
        out_shape=[jax.ShapeDtypeStruct(shape, dtype) for shape, dtype, _, _ in outs],
        grid_spec=pltpu.PrefetchScalarGridSpec(
            num_scalar_prefetch=n_scalar,
            grid=grid,
            in_specs=specs,
            out_specs=[pl.BlockSpec(block, index) for _, _, block, index in outs],
            scratch_shapes=list(scratch),
        ),
        compiler_params=pltpu.CompilerParams(vmem_limit_bytes=LIMITS.get(kernel.__name__, LIMIT) << 20),
        cost_estimate=pl.CostEstimate(flops=cost, bytes_accessed=cost // 300, transcendentals=0),
        name=kernel.__name__,
    )(*([] if scalars is None else [scalars]), *[a for a, _, _ in ins], *deps)


def build_tree(n_dp, n_expert):
    nz, nx, nc, ny = 4, 2, 2, 2

    def along_z(pairs):
        return [(a * nx + x, b * nx + x) for a, b in pairs for x in range(nx)]

    buddy = along_z([(0, 1), (1, 0), (2, 3), (3, 2)])
    middle = along_z([(1, 2), (2, 1)])
    skip = along_z([(0, 2), (2, 0), (1, 3), (3, 1)])
    mirror = along_z([(0, 3), (3, 0), (1, 2), (2, 1)])
    inward = along_z([(0, 1), (3, 2)])
    outward = along_z([(1, 0), (2, 3)])
    swap_x = [(e, e ^ 1) for e in range(n_expert)]
    swap_core = [(d, d ^ 1) for d in range(n_dp)]
    swap_y = [(d, d ^ 2) for d in range(n_dp)]

    def over_expert(a, pairs):
        return lax.ppermute(a, "expert", pairs)

    def over_dp(a, pairs):
        return lax.ppermute(a, "dp", pairs)

    def local(hidden_in, down_weight, routes, gate_prob, cotangent):
        me = lax.axis_index("expert")
        z, x = me // nx, me % nx
        dp = lax.axis_index("dp")
        cap = hidden_in.shape[2] // n_expert
        ff = hidden_in.shape[3]
        tok, top = routes.shape
        features = down_weight.shape[2]
        tile = 512
        tiles = features // tile
        first = (tiles + 1) // 2
        begin, count = (0, first), (first, tiles - first)
        widths = [n * tile for n in count]
        spans = [(b * tile, (b + n) * tile) for b, n in zip(begin, count)]
        half = 2 * cap
        part = ff // n_dp
        last, named = [], []

        def chain(kernel, grid, ins, outs, scratch=(), deps=(), flops=0):
            named.append(kernel.__name__)
            cost = COSTS.get(f"{named[-1]}{named.count(named[-1])}", COST)
            got = call(kernel, grid, ins, outs, scratch, scalars, tuple(last) + tuple(deps), cost)
            last[:] = got[-1:]
            return got[:-1]

        def hold(a, *deps):
            a = after(a, *last, *deps)
            last[:] = [a]
            return a
        blocks_in = hidden_in.reshape(n_expert, cap, ff)
        is_middle = (z == 1) | (z == 2)
        low = z < 2
        order_z = jnp.stack([z, z ^ 1, jnp.where(low, 2, 1), jnp.where(low, 3, 0)])
        order_x = jnp.stack([x, x ^ 1])
        order = (order_z[None, :] * nx + order_x[:, None]).reshape(-1)
        parts = jnp.stack([dp ^ 3, dp ^ 1, dp ^ 2, dp])
        scalars = jnp.concatenate(
            [order, parts, jnp.stack([is_middle.astype(jnp.int32), z * nx + x, z * nx + (x ^ 1)])]
        ).astype(jnp.int32)
        at_parts, at_middle, at_here = n_expert, n_expert + n_dp, n_expert + n_dp + 1

        buddies = over_expert(cotangent, buddy)
        mids = over_expert(cotangent, middle)
        table = jnp.concatenate([routes.astype(F32), gate_prob], axis=1).T

        def whole(a):
            return (a, a.shape, lambda *_: (0,) * a.ndim)

        def sliced(body, fixed):
            def run(s, *refs):
                kept, moving = refs[:fixed], refs[fixed:]
                for k in range(moving[-1].shape[-1] // tile):
                    body(s, *kept, *(ref.at[:, k * tile:(k + 1) * tile] for ref in moving))

            run.__name__ = body.__name__
            return run

        def strip_of(a):
            return (a, a.shape, lambda *_: (0, 0))

        def strip_out(rows, c, dtype=BF16):
            return ((rows, widths[c]), dtype, (rows, widths[c]), lambda *_: (0, 0))

        def columns(a, first=0):
            return (a, (a.shape[0], tile), lambda j, *_: (0, first + j))

        def wide(rows, c, dtype=BF16):
            return ((rows, widths[c]), dtype, (rows, tile), lambda j, *_: (0, j))

        def full(rows, dtype=BF16):
            return ((rows, features), dtype, (rows, tile), lambda j, *_: (0, j))

        broad = features // 4

        def broadly(rows):
            return ((rows, features), BF16, (rows, broad), lambda j, *_: (0, j))

        def product(q):
            def made(s, *refs):
                *given, w, w_low, near_ref, far_ref, rows = refs

                @pl.when(pl.program_id(0) == 0)
                def _():
                    for i, ref in enumerate(given):
                        rows[i * cap:(i + 1) * cap] = ref[0]

                middle_row = ff // 2
                out = dot(rows[:, :middle_row], w[0]) + dot(rows[:, middle_row:], w_low[0])
                near_ref[...] = out[:half].astype(BF16)
                far_ref[...] = out[half:].astype(BF16)

            ins = [
                (blocks_in, (1, cap, ff), lambda j, s, i=i: (s[q * nz + i], 0, 0)) for i in range(nz)
            ]
            for r in range(2):
                ins.append((down_weight, (1, ff // 2, broad), lambda j, s, r=r: (0, r, j)))
            return chain(
                made, (features // broad,), ins, [broadly(half), broadly(half)],
                [pltpu.VMEM((nz * cap, ff), BF16)],
            )

        there_near, there_far = product(1)
        pair = jnp.concatenate([table, over_expert(table, buddy)])
        rs_far = over_expert(there_far, swap_x)

        here_near, here_far = product(0)
        pair = hold(pair)
        far_pair = over_expert(pair, skip)

        def onehot(pos_ref, row):
            slot = lax.broadcasted_iota(jnp.int32, (cap, tok), 0)
            return slot == pos_ref[row:row + 1, :]

        def pack_rows(pos_ref, gate_ref, first, held, send_ref, keep_ref):
            for i, block in enumerate(held):
                for q, ref in enumerate((keep_ref, send_ref)):
                    row = (first + i) * nx + q
                    hot = onehot(pos_ref, row)
                    scale = jnp.sum(
                        jnp.where(hot, gate_ref[row:row + 1, :], 0.0), axis=1, keepdims=True
                    )
                    rows = dot(hot.astype(BF16), block)
                    ref[i * cap:(i + 1) * cap] = (rows * scale).astype(BF16)

        def spread_rows(pos_ref, gate_ref, row, here, there):
            total = None
            for q, rows in enumerate((here, there)):
                at = row * nx + q
                weighted = jnp.where(onehot(pos_ref, at), gate_ref[at:at + 1, :], 0.0).astype(BF16)
                term = lax.dot_general(
                    weighted, rows, (((0,), (0,)), ((), ())), preferred_element_type=F32
                )
                total = term if total is None else total + term
            return total

        def entire(rows, dtype=BF16, cols=None):
            shape = (rows, features if cols is None else cols)
            return (shape, dtype, shape, lambda *_: (0, 0))

        def packed_near(s, pos_ref, gate_ref, own, other, send_ref, keep_ref):
            pack_rows(pos_ref, gate_ref, 0, (own[...], other[...]), send_ref, keep_ref)

        def packed_far(s, pos_ref, gate_ref, m0, o0, m1, o1, first_ref, second_ref, keep_ref):
            middle_here = s[at_middle] == 1
            for k in range(tiles):
                at = slice(k * tile, (k + 1) * tile)
                held = [
                    jnp.where(middle_here, a[:, at], b[:, at]) for a, b in ((m0, o0), (m1, o1))
                ]
                send, moved = (first_ref, 0) if k < first else (second_ref, first)
                send = send.at[:, (k - moved) * tile:(k - moved + 1) * tile]
                pack_rows(pos_ref, gate_ref, 2, held, send, keep_ref.at[:, at])

        def shared_far(s, pos_ref, gate_ref, here, there, far_ref, last_ref):
            for i, ref in enumerate((far_ref, last_ref)):
                lines = slice(i * cap, (i + 1) * cap)
                total = spread_rows(pos_ref, gate_ref, 2 + i, here[lines], there[lines])
                ref[...] = total.astype(BF16)

        def shared_near(s, pos_ref, gate_ref, here, there, sum_ref, keep_ref, send_ref):
            for i, ref in enumerate((keep_ref, send_ref)):
                lines = slice(i * cap, (i + 1) * cap)
                total = spread_rows(pos_ref, gate_ref, i, here[lines], there[lines])
                if i == 1:
                    total = total + sum_ref[...].astype(F32)
                ref[...] = total.astype(ref.dtype)

        def plus(a, b):
            def add(s, a_ref, b_ref, out_ref):
                out_ref[...] = a_ref[...] + b_ref[...]

            return chain(add, (1,), [whole(a), whole(b)], [entire(tok)])[0]

        def turned(s, *refs):
            *given, out_ref, rows = refs

            @pl.when(pl.program_id(0) == 0)
            def _():
                for i, ref in enumerate(given):
                    rows[i * cap:(i + 1) * cap] = ref[0]

            first = pl.multiple_of(s[at_parts + pl.program_id(0)] * part, part)
            out_ref[...] = rows[:, pl.ds(first, part)].T

        slots = n_expert * cap

        mids = hold(mids, buddies)
        mid_last = over_expert(buddies, middle)
        out_far = over_expert(mids, outward)

        def positions(s, near_ref, far_ref, pos_ref, gate_ref):
            middle_here = s[at_middle] == 1
            rows = 2 * top
            held = [
                near_ref[:rows],
                near_ref[rows:],
                jnp.where(middle_here, far_ref[rows:], far_ref[:rows]),
                jnp.where(middle_here, far_ref[:rows], far_ref[rows:]),
            ]
            match, gates = [], []
            for t in held:
                for q in range(nx):
                    named = t[:top] == s[at_here + q].astype(F32)
                    match.append(jnp.sum(named.astype(F32), axis=0, keepdims=True))
                    gates.append(jnp.sum(jnp.where(named, t[top:], 0.0), axis=0, keepdims=True))
            match = jnp.concatenate(match, axis=0)
            earlier = lax.broadcasted_iota(jnp.int32, (tok, tok), 0) < lax.broadcasted_iota(
                jnp.int32, (tok, tok), 1
            )
            before = dot(match.astype(BF16), earlier.astype(BF16))
            pos_ref[...] = jnp.where(match > 0, before, -1.0).astype(jnp.int32)
            gate_ref[...] = jnp.concatenate(gates, axis=0)

        small = (nz * nx, tok)
        pos, gate = chain(
            positions, (1,), [whole(pair), whole(far_pair)],
            [(small, jnp.int32, small, lambda *_: (0, 0)), (small, F32, small, lambda *_: (0, 0))],
        )
        def pieces(c):
            whole_width = [columns(a, begin[c]) for a in (own_near, own_far, ag_near)]
            return whole_width + [columns(ag_far[c])]

        share_rows = ny * part

        def stack_pieces(given, rows):
            for i, ref in enumerate(given):
                rows[i * half:(i + 1) * half] = ref[...]

        def weight_give(c):
            def gave(s, *refs):
                *given, turned_ref, out_ref, rows_ref = refs
                stack_pieces(given, rows_ref)
                out_ref[...] = dot(turned_ref[...], rows_ref[...]).astype(BF16)

            return chain(
                gave, (count[c],),
                pieces(c) + [(hidden_t, (share_rows, slots), lambda *_: (0, 0))],
                [wide(share_rows, c), wide(slots, c)],
            )

        def weight_keep(rows, c, got):
            def kept(s, rows_ref, turned_ref, got_ref, send_ref, keep_ref):
                out = dot(turned_ref[...], rows_ref[...]).astype(BF16).astype(F32)
                out = out + got_ref[...].astype(F32)
                send_ref[...] = out[:part].astype(BF16)
                keep_ref[...] = out[part:]

            return chain(
                kept, (count[c],),
                [columns(rows), (hidden_t, (share_rows, slots), lambda *_: (1, 0)), columns(got)],
                [wide(part, c), wide(part, c, F32)],
            )

        def hidden_all(rows_a, rows_b, deps):
            strip = 256

            def hidden(s, a_ref, b_ref, w, h, out_ref, scalar_ref):
                j = pl.program_id(0)
                total = None
                for ref, (first, end) in zip((a_ref, b_ref), spans):
                    term = lax.dot_general(
                        ref[...], w[0, :, first:end], (((1,), (1,)), ((), ())),
                        preferred_element_type=F32,
                    )
                    total = term if total is None else total + term
                for i in range(n_expert):
                    mine = total[i * cap:(i + 1) * cap]
                    out_ref[s[i]] = mine.astype(BF16)
                    term = jnp.sum(mine * h[s[i]].astype(F32), axis=1, keepdims=True)
                    term = jnp.broadcast_to(term, (cap, 128))

                    @pl.when(j == 0)
                    def _():
                        scalar_ref[i] = term

                    @pl.when(j > 0)
                    def _():
                        scalar_ref[i] += term

            strips = (n_expert, cap, strip)
            return chain(
                hidden, (ff // strip,),
                [
                    whole(rows_a), whole(rows_b),
                    (down_weight, (1, strip, features), lambda j, s: (0, j, 0)),
                    (blocks_in, strips, lambda j, s: (0, 0, j)),
                ],
                [
                    (blocks_in.shape, BF16, strips, lambda j, s: (0, 0, j)),
                    ((n_expert, cap, 128), F32, (n_expert, cap, 128), lambda *_: (0, 0, 0)),
                ],
                (), deps,
            )

        there_near = hold(there_near)
        send, own_near = chain(
            sliced(packed_near, 2), (1,),
            [whole(a) for a in (pos, gate, cotangent, buddies)], [entire(half), entire(half)],
        )
        ag_near = over_expert(send, swap_x)
        rs_near = over_expert(there_near, swap_x)
        (hidden_t,) = chain(
            turned, (n_dp,),
            [(blocks_in, (1, cap, ff), lambda j, s, i=i: (s[i], 0, 0)) for i in range(n_expert)],
            [((ff, slots), BF16, (part, slots), lambda j, *_: (j, 0))],
            [pltpu.VMEM((slots, ff), BF16)],
        )
        sum_far, sum_last = chain(
            sliced(shared_far, 2), (1,),
            [whole(a) for a in (pos, gate, here_far, rs_far)],
            [entire(tok), entire(tok)],
        )
        one = over_expert(sum_last, inward)
        mid_last = hold(mid_last, out_far)
        out_last = over_expert(mid_last, outward)
        rs_near = hold(rs_near)
        two = over_expert(plus(sum_last, one), middle)
        sum_far = hold(sum_far, one)
        one_far = over_expert(sum_far, inward)
        send_a, send_b, own_far = chain(
            packed_far, (1,),
            [whole(a) for a in (pos, gate, mids, out_far, mid_last, out_last)],
            [entire(half, BF16, widths[0]), entire(half, BF16, widths[1]), entire(half)],
        )
        ag_far = [over_expert(send_a, swap_x), over_expert(send_b, swap_x)]
        two_far = over_expert(plus(sum_far, one_far), middle)
        give, rows_a = weight_give(0)
        got = over_dp(give, swap_core)
        keep, give = chain(
            sliced(shared_near, 2), (1,),
            [whole(a) for a in (pos, gate, here_near, rs_near, two)],
            [entire(tok, F32), entire(tok)],
        )
        three = over_expert(give, buddy)
        send_a, keep_a = weight_keep(rows_a, 0, got)
        got_a = over_dp(send_a, swap_y)
        give, rows_b = weight_give(1)
        got = over_dp(give, swap_core)
        hidden_grad, scalar_rows = hidden_all(rows_a, rows_b, ())
        two_far = hold(two_far)
        send_b, keep_b = weight_keep(rows_b, 1, got)
        got_b = over_dp(send_b, swap_y)
        scalar_rows = hold(scalar_rows)
        three = hold(three)
        got_a = hold(got_a)

        def add_three(s, a, b, c, out_ref):
            total = a[...] + b[...].astype(F32) + c[...].astype(F32)
            out_ref[...] = total.astype(BF16)

        (combined,) = chain(
            add_three, (1,), [whole(a) for a in (keep, three, two_far)], [entire(tok)]
        )

        def add_chunks(s, *refs):
            *given, out_ref = refs
            for c in range(2):
                total = given[2 * c][...] + given[2 * c + 1][...].astype(F32)
                out_ref[0, :, spans[c][0]:spans[c][1]] = total.astype(BF16)

        strip = part // 2
        (weight_grad,) = chain(
            add_chunks, (2,),
            [(a, (strip, a.shape[1]), lambda j, *_: (j, 0)) for a in (keep_a, got_a, keep_b, got_b)],
            [((1, part, features), BF16, (1, strip, features), lambda j, *_: (0, j, 0))],
        )

        back = scalar_rows[:, :, 0].reshape(nx, nz, cap)
        back = jnp.stack([back[0], over_expert(back[1], swap_x)], axis=1)
        home = jnp.stack(
            [
                back[0],
                over_expert(back[1], buddy),
                over_expert(jnp.where(is_middle, back[3], back[2]), skip),
                over_expert(jnp.where(is_middle, back[2], back[3]), mirror),
            ]
        ).reshape(n_expert, cap)
        from_z = jnp.stack([z, z ^ 1, z ^ 2, 3 - z])
        ids = (from_z[:, None] * nx + order_x[None, :]).reshape(-1)
        said = routes.T[None] == ids[:, None, None]
        match = said.any(axis=1)
        count = match.astype(jnp.int32)
        before = jnp.cumsum(count, axis=1) - count
        slot = jnp.arange(cap, dtype=jnp.int32)[:, None]
        mine = match[:, None, :] & (before[:, None, :] == slot)
        by_token = jnp.sum(jnp.where(mine, home[:, :, None], 0.0), axis=1)
        gate_grad = jnp.sum(jnp.where(said, by_token[:, None], 0.0), axis=0).T / gate_prob
        return (
            combined,
            gate_grad,
            hidden_grad.reshape(hidden_in.shape),
            weight_grad,
        )

    return local


def build(n_dp, n_expert):
    if split_expert(n_expert) == (4, 2) and n_dp == 4:
        return build_tree(n_dp, n_expert)
    return build_line(n_dp, n_expert)


def solution(mesh):
    in_specs = (
        P("expert", "dp", None, None),
        P("expert", None, None),
        P(("dp", "expert"), None),
        P(("dp", "expert"), None),
        P(("dp", "expert"), None),
    )
    out_specs = (
        P(("dp", "expert"), None),
        P(("dp", "expert"), None),
        P("expert", "dp", None, None),
        P("expert", "dp", None),
    )
    local = build(mesh.shape["dp"], mesh.shape["expert"])
    return jax.shard_map(local, mesh=mesh, in_specs=in_specs, out_specs=out_specs, check_vma=False)
```

```python
import math

import jax
import jax.numpy as jnp
from jax import lax
from jax.experimental import pallas as pl
from jax.experimental.pallas import tpu as pltpu
from jax.sharding import PartitionSpec as P

BF16 = jnp.bfloat16
F32 = jnp.float32
CHUNKS = 2
COST = 10**11
COSTS = {'positions1': 1, 'packed_near1': 1, 'turned1': 1, 'kept2': 1}
LIMIT = 24
LIMITS = {'hidden': 40, 'made': 60}


def split_expert(n):
    nx = 1
    while nx * nx * 4 <= n:
        nx *= 2
    while n % nx:
        nx -= 1
    return n // nx, nx


def dot(a, b):
    return jnp.dot(a, b, preferred_element_type=F32)


def build_line(n_dp, n_expert):
    nz, nx = split_expert(n_expert)
    nc = 2 if n_dp % 2 == 0 else 1
    ny = n_dp // nc

    def along_z(move):
        return [
            (z * nx + x, move(z) * nx + x)
            for z in range(nz)
            for x in range(nx)
            if move(z) is not None
        ]

    def shift_z(r):
        return along_z(lambda z: (z + r) % nz)

    def line(step, first, last):
        return along_z(lambda z: z + step if first <= z <= last and 0 <= z + step < nz else None)

    def shift_x(q):
        return [(z * nx + x, z * nx + (x + q) % nx) for z in range(nz) for x in range(nx)]

    def shift_y(o):
        return [(y * nc + c, (y + o) % ny * nc + c) for y in range(ny) for c in range(nc)]

    swap_core = [(y * nc + c, y * nc + (c + 1) % nc) for y in range(ny) for c in range(nc)]

    def over_expert(a, pairs):
        return lax.ppermute(a, "expert", pairs)

    def over_dp(a, pairs):
        return lax.ppermute(a, "dp", pairs)

    def local(hidden_in, down_weight, routes, gate_prob, cotangent):
        me = lax.axis_index("expert")
        z, x = me // nx, me % nx
        dp = lax.axis_index("dp")
        y, core = dp // nc, dp % nc
        cap = hidden_in.shape[2] // n_expert
        ff = hidden_in.shape[3]
        tok, top = routes.shape
        features = down_weight.shape[2]
        width = features // CHUNKS
        weight = down_weight[0]

        table = jnp.concatenate([routes.astype(F32), gate_prob], axis=1).T
        tables = jnp.stack([table] + [over_expert(table, shift_z(r)) for r in range(1, nz)])
        line_routes = tables[:, :top].astype(jnp.int32)
        line_gates = tables[:, top:]
        here = z * nx + (x + jnp.arange(nx, dtype=jnp.int32)) % nx

        def slots_of(routed, ids):
            named = routed[..., None, :, :] == ids[:, None, None]
            match = named.any(axis=-2)
            count = match.astype(jnp.int32)
            before = jnp.cumsum(count, axis=-1) - count
            slot = jnp.arange(cap, dtype=jnp.int32)[:, None]
            onehot = match[..., None, :] & (before[..., None, :] == slot)
            return onehot, named

        onehot, named = slots_of(line_routes, here)
        token_gate = jnp.sum(jnp.where(named, line_gates[:, None], 0.0), axis=-2)
        slot_gate = jnp.sum(jnp.where(onehot, token_gate[..., None, :], 0.0), axis=-1)
        pick = onehot.astype(BF16).reshape(nz, nx * cap, tok)
        spread = jnp.where(onehot, token_gate[..., None, :], 0.0).astype(BF16)
        spread = spread.reshape(nz, nx * cap, tok)
        slot_gate = slot_gate.reshape(nz, nx * cap, 1)

        blocks = hidden_in.reshape(nz, nx, cap, ff)
        order_z = (z - jnp.arange(nz)) % nz
        order_x = (x + jnp.arange(nx)) % nx
        hidden = blocks[order_z][:, order_x].transpose(1, 0, 2, 3).reshape(-1, ff)

        rows = ff // n_dp
        hidden_t = hidden.T.reshape(ny, nc, rows, -1)
        hidden_t = hidden_t[(y + 1 + jnp.arange(ny)) % ny][:, (core + 1 + jnp.arange(nc)) % nc]
        hidden_t = hidden_t.transpose(1, 0, 2, 3).reshape(nc, ny * rows, -1)

        line_rows = nz * cap

        def dispatch(cot):
            low, high = [cot], [cot]
            for k in range(1, nz):
                low.append(over_expert(low[-1], line(1, k - 1, nz - 2)))
                high.append(over_expert(high[-1], line(-1, 1, nz - k)))
            held = [cot] + [jnp.where(z >= r, low[r], high[nz - r]) for r in range(1, nz)]
            held = jnp.stack(held)
            packed = lax.dot_general(
                pick, held, (((2,), (1,)), ((0,), (0,))), preferred_element_type=F32
            )
            packed = (packed * slot_gate).astype(BF16).reshape(nz, nx, cap, -1)
            out = [packed[:, 0].reshape(line_rows, -1)]
            for q in range(1, nx):
                out.append(over_expert(packed[:, q].reshape(line_rows, -1), shift_x(q)))
            return [out[-q % nx] for q in range(nx)]

        def combine(weight_c):
            produced = dot(hidden, weight_c).astype(BF16).reshape(nx, line_rows, -1)
            got = [produced[0]]
            for q in range(1, nx):
                got.append(over_expert(produced[q], shift_x(q)))
            rows_in = jnp.stack([got[-q % nx].reshape(nz, cap, -1) for q in range(nx)], axis=1)
            rows_in = rows_in.reshape(nz, nx * cap, -1)
            part = lax.dot_general(
                spread, rows_in, (((1,), (1,)), ((0,), (0,))), preferred_element_type=F32
            ).astype(BF16)
            up, down = None, None
            for k in range(1, nz):
                mine = part[k] if up is None else part[k] + up
                up = over_expert(mine, line(1, 0, k - 1))
                mine = part[nz - k] if down is None else part[nz - k] + down
                down = over_expert(mine, line(-1, nz - k, nz - 1))
            total = part[0].astype(F32)
            for other in (up, down):
                if other is not None:
                    total = total + other.astype(F32)
            return total.astype(BF16)

        def weight_part(slot_rows):
            give = dot(hidden_t[0], slot_rows).astype(BF16)
            if nc == 2:
                got = over_dp(give, swap_core)
                keep = dot(hidden_t[1], slot_rows).astype(BF16)
                keep = (keep.astype(F32) + got.astype(F32)).astype(BF16)
            else:
                keep = give
            keep = keep.reshape(ny, rows, -1)
            total = keep[ny - 1].astype(F32)
            for o in range(1, ny):
                total = total + over_dp(keep[o - 1], shift_y(o)).astype(F32)
            return total.astype(BF16)

        combined, weight_grad, slot_grads = [], [], []
        for c in range(CHUNKS):
            columns = slice(c * width, (c + 1) * width)
            slot_rows = jnp.concatenate(dispatch(cotangent[:, columns]), axis=0)
            slot_grads.append(slot_rows)
            combined.append(combine(weight[:, columns]))
            weight_grad.append(weight_part(slot_rows))

        hidden_grad = 0.0
        for c in range(CHUNKS):
            columns = slice(c * width, (c + 1) * width)
            hidden_grad = hidden_grad + lax.dot_general(
                slot_grads[c], weight[:, columns], (((1,), (1,)), ((), ())),
                preferred_element_type=F32,
            )
        scalars = jnp.sum(hidden_grad * hidden.astype(F32), axis=1).reshape(nx, line_rows)
        out = hidden_grad.astype(BF16).reshape(nx, nz, cap, ff)
        out = out[(jnp.arange(nx) - x) % nx][:, (z - jnp.arange(nz)) % nz]
        out = out.transpose(1, 0, 2, 3).reshape(hidden_in.shape)

        back = [scalars[0]] + [over_expert(scalars[q], shift_x(q)) for q in range(1, nx)]
        back = jnp.stack(back).reshape(nx, nz, cap)
        home = [back[:, 0]] + [over_expert(back[:, r], shift_z(-r)) for r in range(1, nz)]
        home = jnp.stack(home).reshape(n_expert, cap)
        far_z = (z + jnp.arange(nz, dtype=jnp.int32)) % nz
        far_x = (x - jnp.arange(nx, dtype=jnp.int32)) % nx
        ids = (far_z[:, None] * nx + far_x[None, :]).reshape(-1)
        mine, said = slots_of(routes.T, ids)
        by_token = jnp.sum(jnp.where(mine, home[:, :, None], 0.0), axis=1)
        gate_grad = jnp.sum(jnp.where(said, by_token[:, None], 0.0), axis=0).T / gate_prob
        return (
            jnp.concatenate(combined, axis=1),
            gate_grad,
            out,
            jnp.concatenate(weight_grad, axis=1)[None],
        )

    return local


def nothing(*refs):
    pass


def after(x, *deps):
    anywhere = pl.BlockSpec(memory_space=pl.ANY)
    return pl.pallas_call(
        nothing,
        out_shape=jax.ShapeDtypeStruct(x.shape, x.dtype),
        in_specs=[anywhere] * (1 + len(deps)),
        out_specs=anywhere,
        input_output_aliases={0: 0},
        name="after",
    )(x, *deps)


def call(kernel, grid, ins, outs, scratch, scalars, deps, cost):
    n_in, n_dep = len(ins), len(deps)
    n_scalar = 0 if scalars is None else 1

    def body(*refs):
        first, end = n_scalar + n_in, n_scalar + n_in + n_dep + len(outs) - 1
        refs[end][...] = jnp.zeros((8, 128), F32)
        kernel(*refs[:first], *refs[first + n_dep:end], *refs[end + 1:])

    outs = list(outs) + [((8, 128), F32, (8, 128), lambda *_: (0, 0))]

    specs = [pl.BlockSpec(block, index) for _, block, index in ins]
    specs += [pl.BlockSpec(memory_space=pl.ANY)] * n_dep
    return pl.pallas_call(
        body,
        out_shape=[jax.ShapeDtypeStruct(shape, dtype) for shape, dtype, _, _ in outs],
        grid_spec=pltpu.PrefetchScalarGridSpec(
            num_scalar_prefetch=n_scalar,
            grid=grid,
            in_specs=specs,
            out_specs=[pl.BlockSpec(block, index) for _, _, block, index in outs],
            scratch_shapes=list(scratch),
        ),
        compiler_params=pltpu.CompilerParams(vmem_limit_bytes=LIMITS.get(kernel.__name__, LIMIT) << 20),
        cost_estimate=pl.CostEstimate(flops=cost, bytes_accessed=cost // 300, transcendentals=0),
        name=kernel.__name__,
    )(*([] if scalars is None else [scalars]), *[a for a, _, _ in ins], *deps)


def build_tree(n_dp, n_expert):
    nz, nx, nc, ny = 4, 2, 2, 2

    def along_z(pairs):
        return [(a * nx + x, b * nx + x) for a, b in pairs for x in range(nx)]

    buddy = along_z([(0, 1), (1, 0), (2, 3), (3, 2)])
    middle = along_z([(1, 2), (2, 1)])
    skip = along_z([(0, 2), (2, 0), (1, 3), (3, 1)])
    mirror = along_z([(0, 3), (3, 0), (1, 2), (2, 1)])
    inward = along_z([(0, 1), (3, 2)])
    outward = along_z([(1, 0), (2, 3)])
    swap_x = [(e, e ^ 1) for e in range(n_expert)]
    swap_core = [(d, d ^ 1) for d in range(n_dp)]
    swap_y = [(d, d ^ 2) for d in range(n_dp)]

    def over_expert(a, pairs):
        return lax.ppermute(a, "expert", pairs)

    def over_dp(a, pairs):
        return lax.ppermute(a, "dp", pairs)

    def local(hidden_in, down_weight, routes, gate_prob, cotangent):
        me = lax.axis_index("expert")
        z, x = me // nx, me % nx
        dp = lax.axis_index("dp")
        cap = hidden_in.shape[2] // n_expert
        ff = hidden_in.shape[3]
        tok, top = routes.shape
        features = down_weight.shape[2]
        tile = 512
        tiles = features // tile
        first = (tiles + 1) // 2
        begin, count = (0, first), (first, tiles - first)
        widths = [n * tile for n in count]
        spans = [(b * tile, (b + n) * tile) for b, n in zip(begin, count)]
        half = 2 * cap
        part = ff // n_dp
        last, named = [], []

        def chain(kernel, grid, ins, outs, scratch=(), deps=(), flops=0):
            named.append(kernel.__name__)
            cost = COSTS.get(f"{named[-1]}{named.count(named[-1])}", COST)
            got = call(kernel, grid, ins, outs, scratch, scalars, tuple(last) + tuple(deps), cost)
            last[:] = got[-1:]
            return got[:-1]

        def hold(a, *deps):
            a = after(a, *last, *deps)
            last[:] = [a]
            return a
        blocks_in = hidden_in.reshape(n_expert, cap, ff)
        is_middle = (z == 1) | (z == 2)
        low = z < 2
        order_z = jnp.stack([z, z ^ 1, jnp.where(low, 2, 1), jnp.where(low, 3, 0)])
        order_x = jnp.stack([x, x ^ 1])
        order = (order_z[None, :] * nx + order_x[:, None]).reshape(-1)
        parts = jnp.stack([dp ^ 3, dp ^ 1, dp ^ 2, dp])
        scalars = jnp.concatenate(
            [order, parts, jnp.stack([is_middle.astype(jnp.int32), z * nx + x, z * nx + (x ^ 1)])]
        ).astype(jnp.int32)
        at_parts, at_middle, at_here = n_expert, n_expert + n_dp, n_expert + n_dp + 1

        buddies = over_expert(cotangent, buddy)
        mids = over_expert(cotangent, middle)
        table = jnp.concatenate([routes.astype(F32), gate_prob], axis=1).T

        def whole(a):
            return (a, a.shape, lambda *_: (0,) * a.ndim)

        def sliced(body, fixed):
            def run(s, *refs):
                kept, moving = refs[:fixed], refs[fixed:]
                for k in range(moving[-1].shape[-1] // tile):
                    body(s, *kept, *(ref.at[:, k * tile:(k + 1) * tile] for ref in moving))

            run.__name__ = body.__name__
            return run

        def strip_of(a):
            return (a, a.shape, lambda *_: (0, 0))

        def strip_out(rows, c, dtype=BF16):
            return ((rows, widths[c]), dtype, (rows, widths[c]), lambda *_: (0, 0))

        def columns(a, first=0):
            return (a, (a.shape[0], tile), lambda j, *_: (0, first + j))

        def wide(rows, c, dtype=BF16):
            return ((rows, widths[c]), dtype, (rows, tile), lambda j, *_: (0, j))

        def full(rows, dtype=BF16):
            return ((rows, features), dtype, (rows, tile), lambda j, *_: (0, j))

        broad = features // 4

        def broadly(rows):
            return ((rows, features), BF16, (rows, broad), lambda j, *_: (0, j))

        def product(q):
            def made(s, *refs):
                *given, w, w_low, near_ref, far_ref, rows = refs

                @pl.when(pl.program_id(0) == 0)
                def _():
                    for i, ref in enumerate(given):
                        rows[i * cap:(i + 1) * cap] = ref[0]

                middle_row = ff // 2
                out = dot(rows[:, :middle_row], w[0]) + dot(rows[:, middle_row:], w_low[0])
                near_ref[...] = out[:half].astype(BF16)
                far_ref[...] = out[half:].astype(BF16)

            ins = [
                (blocks_in, (1, cap, ff), lambda j, s, i=i: (s[q * nz + i], 0, 0)) for i in range(nz)
            ]
            for r in range(2):
                ins.append((down_weight, (1, ff // 2, broad), lambda j, s, r=r: (0, r, j)))
            return chain(
                made, (features // broad,), ins, [broadly(half), broadly(half)],
                [pltpu.VMEM((nz * cap, ff), BF16)],
            )

        there_near, there_far = product(1)
        pair = jnp.concatenate([table, over_expert(table, buddy)])
        rs_far = over_expert(there_far, swap_x)

        here_near, here_far = product(0)
        pair = hold(pair)
        far_pair = over_expert(pair, skip)

        def onehot(pos_ref, row):
            slot = lax.broadcasted_iota(jnp.int32, (cap, tok), 0)
            return slot == pos_ref[row:row + 1, :]

        def pack_rows(pos_ref, gate_ref, first, held, send_ref, keep_ref):
            for i, block in enumerate(held):
                for q, ref in enumerate((keep_ref, send_ref)):
                    row = (first + i) * nx + q
                    hot = onehot(pos_ref, row)
                    scale = jnp.sum(
                        jnp.where(hot, gate_ref[row:row + 1, :], 0.0), axis=1, keepdims=True
                    )
                    rows = dot(hot.astype(BF16), block)
                    ref[i * cap:(i + 1) * cap] = (rows * scale).astype(BF16)

        def spread_rows(pos_ref, gate_ref, row, here, there):
            total = None
            for q, rows in enumerate((here, there)):
                at = row * nx + q
                weighted = jnp.where(onehot(pos_ref, at), gate_ref[at:at + 1, :], 0.0).astype(BF16)
                term = lax.dot_general(
                    weighted, rows, (((0,), (0,)), ((), ())), preferred_element_type=F32
                )
                total = term if total is None else total + term
            return total

        def entire(rows, dtype=BF16, cols=None):
            shape = (rows, features if cols is None else cols)
            return (shape, dtype, shape, lambda *_: (0, 0))

        def packed_near(s, pos_ref, gate_ref, own, other, send_ref, keep_ref):
            pack_rows(pos_ref, gate_ref, 0, (own[...], other[...]), send_ref, keep_ref)

        def packed_far(s, pos_ref, gate_ref, m0, o0, m1, o1, first_ref, second_ref, keep_ref):
            middle_here = s[at_middle] == 1
            for k in range(tiles):
                at = slice(k * tile, (k + 1) * tile)
                held = [
                    jnp.where(middle_here, a[:, at], b[:, at]) for a, b in ((m0, o0), (m1, o1))
                ]
                send, moved = (first_ref, 0) if k < first else (second_ref, first)
                send = send.at[:, (k - moved) * tile:(k - moved + 1) * tile]
                pack_rows(pos_ref, gate_ref, 2, held, send, keep_ref.at[:, at])

        def shared_far(s, pos_ref, gate_ref, here, there, far_ref, last_ref):
            for i, ref in enumerate((far_ref, last_ref)):
                lines = slice(i * cap, (i + 1) * cap)
                total = spread_rows(pos_ref, gate_ref, 2 + i, here[lines], there[lines])
                ref[...] = total.astype(BF16)

        def shared_near(s, pos_ref, gate_ref, here, there, sum_ref, keep_ref, send_ref):
            for i, ref in enumerate((keep_ref, send_ref)):
                lines = slice(i * cap, (i + 1) * cap)
                total = spread_rows(pos_ref, gate_ref, i, here[lines], there[lines])
                if i == 1:
                    total = total + sum_ref[...].astype(F32)
                ref[...] = total.astype(ref.dtype)

        def plus(a, b):
            def add(s, a_ref, b_ref, out_ref):
                out_ref[...] = a_ref[...] + b_ref[...]

            return chain(add, (1,), [whole(a), whole(b)], [entire(tok)])[0]

        def turned(s, *refs):
            *given, out_ref, rows = refs

            @pl.when(pl.program_id(0) == 0)
            def _():
                for i, ref in enumerate(given):
                    rows[i * cap:(i + 1) * cap] = ref[0]

            first = pl.multiple_of(s[at_parts + pl.program_id(0)] * part, part)
            out_ref[...] = rows[:, pl.ds(first, part)].T

        slots = n_expert * cap

        buddies = hold(buddies)
        mid_last = over_expert(buddies, middle)
        mids = hold(mids)
        out_far = over_expert(mids, outward)

        def positions(s, near_ref, far_ref, pos_ref, gate_ref):
            middle_here = s[at_middle] == 1
            rows = 2 * top
            held = [
                near_ref[:rows],
                near_ref[rows:],
                jnp.where(middle_here, far_ref[rows:], far_ref[:rows]),
                jnp.where(middle_here, far_ref[:rows], far_ref[rows:]),
            ]
            match, gates = [], []
            for t in held:
                for q in range(nx):
                    named = t[:top] == s[at_here + q].astype(F32)
                    match.append(jnp.sum(named.astype(F32), axis=0, keepdims=True))
                    gates.append(jnp.sum(jnp.where(named, t[top:], 0.0), axis=0, keepdims=True))
            match = jnp.concatenate(match, axis=0)
            earlier = lax.broadcasted_iota(jnp.int32, (tok, tok), 0) < lax.broadcasted_iota(
                jnp.int32, (tok, tok), 1
            )
            before = dot(match.astype(BF16), earlier.astype(BF16))
            pos_ref[...] = jnp.where(match > 0, before, -1.0).astype(jnp.int32)
            gate_ref[...] = jnp.concatenate(gates, axis=0)

        small = (nz * nx, tok)
        pos, gate = chain(
            positions, (1,), [whole(pair), whole(far_pair)],
            [(small, jnp.int32, small, lambda *_: (0, 0)), (small, F32, small, lambda *_: (0, 0))],
        )
        def pieces(c):
            whole_width = [columns(a, begin[c]) for a in (own_near, own_far, ag_near)]
            return whole_width + [columns(ag_far[c])]

        share_rows = ny * part

        def stack_pieces(given, rows):
            for i, ref in enumerate(given):
                rows[i * half:(i + 1) * half] = ref[...]

        def weight_give(c):
            def gave(s, *refs):
                *given, turned_ref, out_ref, rows_ref = refs
                stack_pieces(given, rows_ref)
                out_ref[...] = dot(turned_ref[...], rows_ref[...]).astype(BF16)

            return chain(
                gave, (count[c],),
                pieces(c) + [(hidden_t, (share_rows, slots), lambda *_: (0, 0))],
                [wide(share_rows, c), wide(slots, c)],
            )

        def weight_keep(rows, c, got):
            def kept(s, rows_ref, turned_ref, got_ref, send_ref, keep_ref):
                out = dot(turned_ref[...], rows_ref[...]).astype(BF16).astype(F32)
                out = out + got_ref[...].astype(F32)
                send_ref[...] = out[:part].astype(BF16)
                keep_ref[...] = out[part:]

            return chain(
                kept, (count[c],),
                [columns(rows), (hidden_t, (share_rows, slots), lambda *_: (1, 0)), columns(got)],
                [wide(part, c), wide(part, c, F32)],
            )

        def hidden_all(rows_a, rows_b, deps):
            strip = 256

            def hidden(s, a_ref, b_ref, w, h, out_ref, scalar_ref):
                j = pl.program_id(0)
                total = None
                for ref, (first, end) in zip((a_ref, b_ref), spans):
                    term = lax.dot_general(
                        ref[...], w[0, :, first:end], (((1,), (1,)), ((), ())),
                        preferred_element_type=F32,
                    )
                    total = term if total is None else total + term
                for i in range(n_expert):
                    mine = total[i * cap:(i + 1) * cap]
                    out_ref[s[i]] = mine.astype(BF16)
                    term = jnp.sum(mine * h[s[i]].astype(F32), axis=1, keepdims=True)
                    term = jnp.broadcast_to(term, (cap, 128))

                    @pl.when(j == 0)
                    def _():
                        scalar_ref[i] = term

                    @pl.when(j > 0)
                    def _():
                        scalar_ref[i] += term

            strips = (n_expert, cap, strip)
            return chain(
                hidden, (ff // strip,),
                [
                    whole(rows_a), whole(rows_b),
                    (down_weight, (1, strip, features), lambda j, s: (0, j, 0)),
                    (blocks_in, strips, lambda j, s: (0, 0, j)),
                ],
                [
                    (blocks_in.shape, BF16, strips, lambda j, s: (0, 0, j)),
                    ((n_expert, cap, 128), F32, (n_expert, cap, 128), lambda *_: (0, 0, 0)),
                ],
                (), deps,
            )

        there_near = hold(there_near)
        send, own_near = chain(
            sliced(packed_near, 2), (1,),
            [whole(a) for a in (pos, gate, cotangent, buddies)], [entire(half), entire(half)],
        )
        ag_near = over_expert(send, swap_x)
        rs_near = over_expert(there_near, swap_x)
        (hidden_t,) = chain(
            turned, (n_dp,),
            [(blocks_in, (1, cap, ff), lambda j, s, i=i: (s[i], 0, 0)) for i in range(n_expert)],
            [((ff, slots), BF16, (part, slots), lambda j, *_: (j, 0))],
            [pltpu.VMEM((slots, ff), BF16)],
        )
        sum_far, sum_last = chain(
            sliced(shared_far, 2), (1,),
            [whole(a) for a in (pos, gate, here_far, rs_far)],
            [entire(tok), entire(tok)],
        )
        one = over_expert(sum_last, inward)
        mid_last = hold(mid_last, out_far)
        out_last = over_expert(mid_last, outward)
        rs_near = hold(rs_near)
        two = over_expert(plus(sum_last, one), middle)
        sum_far = hold(sum_far, one)
        one_far = over_expert(sum_far, inward)
        send_a, send_b, own_far = chain(
            packed_far, (1,),
            [whole(a) for a in (pos, gate, mids, out_far, mid_last, out_last)],
            [entire(half, BF16, widths[0]), entire(half, BF16, widths[1]), entire(half)],
        )
        ag_far = [over_expert(send_a, swap_x), over_expert(send_b, swap_x)]
        two_far = over_expert(plus(sum_far, one_far), middle)
        give, rows_a = weight_give(0)
        got = over_dp(give, swap_core)
        keep, give = chain(
            sliced(shared_near, 2), (1,),
            [whole(a) for a in (pos, gate, here_near, rs_near, two)],
            [entire(tok, F32), entire(tok)],
        )
        three = over_expert(give, buddy)
        send_a, keep_a = weight_keep(rows_a, 0, got)
        got_a = over_dp(send_a, swap_y)
        give, rows_b = weight_give(1)
        got = over_dp(give, swap_core)
        hidden_grad, scalar_rows = hidden_all(rows_a, rows_b, ())
        two_far = hold(two_far)
        send_b, keep_b = weight_keep(rows_b, 1, got)
        got_b = over_dp(send_b, swap_y)
        scalar_rows = hold(scalar_rows)
        three = hold(three)
        got_a = hold(got_a)

        def add_three(s, a, b, c, out_ref):
            total = a[...] + b[...].astype(F32) + c[...].astype(F32)
            out_ref[...] = total.astype(BF16)

        (combined,) = chain(
            add_three, (1,), [whole(a) for a in (keep, three, two_far)], [entire(tok)]
        )

        def add_chunks(s, *refs):
            *given, out_ref = refs
            for c in range(2):
                total = given[2 * c][...] + given[2 * c + 1][...].astype(F32)
                out_ref[0, :, spans[c][0]:spans[c][1]] = total.astype(BF16)

        strip = part // 2
        (weight_grad,) = chain(
            add_chunks, (2,),
            [(a, (strip, a.shape[1]), lambda j, *_: (j, 0)) for a in (keep_a, got_a, keep_b, got_b)],
            [((1, part, features), BF16, (1, strip, features), lambda j, *_: (0, j, 0))],
        )

        back = scalar_rows[:, :, 0].reshape(nx, nz, cap)
        back = jnp.stack([back[0], over_expert(back[1], swap_x)], axis=1)
        home = jnp.stack(
            [
                back[0],
                over_expert(back[1], buddy),
                over_expert(jnp.where(is_middle, back[3], back[2]), skip),
                over_expert(jnp.where(is_middle, back[2], back[3]), mirror),
            ]
        ).reshape(n_expert, cap)
        from_z = jnp.stack([z, z ^ 1, z ^ 2, 3 - z])
        ids = (from_z[:, None] * nx + order_x[None, :]).reshape(-1)
        said = routes.T[None] == ids[:, None, None]
        match = said.any(axis=1)
        count = match.astype(jnp.int32)
        before = jnp.cumsum(count, axis=1) - count
        slot = jnp.arange(cap, dtype=jnp.int32)[:, None]
        mine = match[:, None, :] & (before[:, None, :] == slot)
        by_token = jnp.sum(jnp.where(mine, home[:, :, None], 0.0), axis=1)
        gate_grad = jnp.sum(jnp.where(said, by_token[:, None], 0.0), axis=0).T / gate_prob
        return (
            combined,
            gate_grad,
            hidden_grad.reshape(hidden_in.shape),
            weight_grad,
        )

    return local


def build(n_dp, n_expert):
    if split_expert(n_expert) == (4, 2) and n_dp == 4:
        return build_tree(n_dp, n_expert)
    return build_line(n_dp, n_expert)


def solution(mesh):
    in_specs = (
        P("expert", "dp", None, None),
        P("expert", None, None),
        P(("dp", "expert"), None),
        P(("dp", "expert"), None),
        P(("dp", "expert"), None),
    )
    out_specs = (
        P(("dp", "expert"), None),
        P(("dp", "expert"), None),
        P("expert", "dp", None, None),
        P("expert", "dp", None),
    )
    local = build(mesh.shape["dp"], mesh.shape["expert"])
    return jax.shard_map(local, mesh=mesh, in_specs=in_specs, out_specs=out_specs, check_vma=False)
```

```python
import math

import jax
import jax.numpy as jnp
from jax import lax
from jax.experimental import pallas as pl
from jax.experimental.pallas import tpu as pltpu
from jax.sharding import PartitionSpec as P

BF16 = jnp.bfloat16
F32 = jnp.float32
CHUNKS = 2
COST = 10**11
COSTS = {'positions1': 1, 'packed_near1': 1, 'turned1': 1, 'kept2': 1}
LIMIT = 24
LIMITS = {'hidden': 40, 'made': 40}


def split_expert(n):
    nx = 1
    while nx * nx * 4 <= n:
        nx *= 2
    while n % nx:
        nx -= 1
    return n // nx, nx


def dot(a, b):
    return jnp.dot(a, b, preferred_element_type=F32)


def build_line(n_dp, n_expert):
    nz, nx = split_expert(n_expert)
    nc = 2 if n_dp % 2 == 0 else 1
    ny = n_dp // nc

    def along_z(move):
        return [
            (z * nx + x, move(z) * nx + x)
            for z in range(nz)
            for x in range(nx)
            if move(z) is not None
        ]

    def shift_z(r):
        return along_z(lambda z: (z + r) % nz)

    def line(step, first, last):
        return along_z(lambda z: z + step if first <= z <= last and 0 <= z + step < nz else None)

    def shift_x(q):
        return [(z * nx + x, z * nx + (x + q) % nx) for z in range(nz) for x in range(nx)]

    def shift_y(o):
        return [(y * nc + c, (y + o) % ny * nc + c) for y in range(ny) for c in range(nc)]

    swap_core = [(y * nc + c, y * nc + (c + 1) % nc) for y in range(ny) for c in range(nc)]

    def over_expert(a, pairs):
        return lax.ppermute(a, "expert", pairs)

    def over_dp(a, pairs):
        return lax.ppermute(a, "dp", pairs)

    def local(hidden_in, down_weight, routes, gate_prob, cotangent):
        me = lax.axis_index("expert")
        z, x = me // nx, me % nx
        dp = lax.axis_index("dp")
        y, core = dp // nc, dp % nc
        cap = hidden_in.shape[2] // n_expert
        ff = hidden_in.shape[3]
        tok, top = routes.shape
        features = down_weight.shape[2]
        width = features // CHUNKS
        weight = down_weight[0]

        table = jnp.concatenate([routes.astype(F32), gate_prob], axis=1).T
        tables = jnp.stack([table] + [over_expert(table, shift_z(r)) for r in range(1, nz)])
        line_routes = tables[:, :top].astype(jnp.int32)
        line_gates = tables[:, top:]
        here = z * nx + (x + jnp.arange(nx, dtype=jnp.int32)) % nx

        def slots_of(routed, ids):
            named = routed[..., None, :, :] == ids[:, None, None]
            match = named.any(axis=-2)
            count = match.astype(jnp.int32)
            before = jnp.cumsum(count, axis=-1) - count
            slot = jnp.arange(cap, dtype=jnp.int32)[:, None]
            onehot = match[..., None, :] & (before[..., None, :] == slot)
            return onehot, named

        onehot, named = slots_of(line_routes, here)
        token_gate = jnp.sum(jnp.where(named, line_gates[:, None], 0.0), axis=-2)
        slot_gate = jnp.sum(jnp.where(onehot, token_gate[..., None, :], 0.0), axis=-1)
        pick = onehot.astype(BF16).reshape(nz, nx * cap, tok)
        spread = jnp.where(onehot, token_gate[..., None, :], 0.0).astype(BF16)
        spread = spread.reshape(nz, nx * cap, tok)
        slot_gate = slot_gate.reshape(nz, nx * cap, 1)

        blocks = hidden_in.reshape(nz, nx, cap, ff)
        order_z = (z - jnp.arange(nz)) % nz
        order_x = (x + jnp.arange(nx)) % nx
        hidden = blocks[order_z][:, order_x].transpose(1, 0, 2, 3).reshape(-1, ff)

        rows = ff // n_dp
        hidden_t = hidden.T.reshape(ny, nc, rows, -1)
        hidden_t = hidden_t[(y + 1 + jnp.arange(ny)) % ny][:, (core + 1 + jnp.arange(nc)) % nc]
        hidden_t = hidden_t.transpose(1, 0, 2, 3).reshape(nc, ny * rows, -1)

        line_rows = nz * cap

        def dispatch(cot):
            low, high = [cot], [cot]
            for k in range(1, nz):
                low.append(over_expert(low[-1], line(1, k - 1, nz - 2)))
                high.append(over_expert(high[-1], line(-1, 1, nz - k)))
            held = [cot] + [jnp.where(z >= r, low[r], high[nz - r]) for r in range(1, nz)]
            held = jnp.stack(held)
            packed = lax.dot_general(
                pick, held, (((2,), (1,)), ((0,), (0,))), preferred_element_type=F32
            )
            packed = (packed * slot_gate).astype(BF16).reshape(nz, nx, cap, -1)
            out = [packed[:, 0].reshape(line_rows, -1)]
            for q in range(1, nx):
                out.append(over_expert(packed[:, q].reshape(line_rows, -1), shift_x(q)))
            return [out[-q % nx] for q in range(nx)]

        def combine(weight_c):
            produced = dot(hidden, weight_c).astype(BF16).reshape(nx, line_rows, -1)
            got = [produced[0]]
            for q in range(1, nx):
                got.append(over_expert(produced[q], shift_x(q)))
            rows_in = jnp.stack([got[-q % nx].reshape(nz, cap, -1) for q in range(nx)], axis=1)
            rows_in = rows_in.reshape(nz, nx * cap, -1)
            part = lax.dot_general(
                spread, rows_in, (((1,), (1,)), ((0,), (0,))), preferred_element_type=F32
            ).astype(BF16)
            up, down = None, None
            for k in range(1, nz):
                mine = part[k] if up is None else part[k] + up
                up = over_expert(mine, line(1, 0, k - 1))
                mine = part[nz - k] if down is None else part[nz - k] + down
                down = over_expert(mine, line(-1, nz - k, nz - 1))
            total = part[0].astype(F32)
            for other in (up, down):
                if other is not None:
                    total = total + other.astype(F32)
            return total.astype(BF16)

        def weight_part(slot_rows):
            give = dot(hidden_t[0], slot_rows).astype(BF16)
            if nc == 2:
                got = over_dp(give, swap_core)
                keep = dot(hidden_t[1], slot_rows).astype(BF16)
                keep = (keep.astype(F32) + got.astype(F32)).astype(BF16)
            else:
                keep = give
            keep = keep.reshape(ny, rows, -1)
            total = keep[ny - 1].astype(F32)
            for o in range(1, ny):
                total = total + over_dp(keep[o - 1], shift_y(o)).astype(F32)
            return total.astype(BF16)

        combined, weight_grad, slot_grads = [], [], []
        for c in range(CHUNKS):
            columns = slice(c * width, (c + 1) * width)
            slot_rows = jnp.concatenate(dispatch(cotangent[:, columns]), axis=0)
            slot_grads.append(slot_rows)
            combined.append(combine(weight[:, columns]))
            weight_grad.append(weight_part(slot_rows))

        hidden_grad = 0.0
        for c in range(CHUNKS):
            columns = slice(c * width, (c + 1) * width)
            hidden_grad = hidden_grad + lax.dot_general(
                slot_grads[c], weight[:, columns], (((1,), (1,)), ((), ())),
                preferred_element_type=F32,
            )
        scalars = jnp.sum(hidden_grad * hidden.astype(F32), axis=1).reshape(nx, line_rows)
        out = hidden_grad.astype(BF16).reshape(nx, nz, cap, ff)
        out = out[(jnp.arange(nx) - x) % nx][:, (z - jnp.arange(nz)) % nz]
        out = out.transpose(1, 0, 2, 3).reshape(hidden_in.shape)

        back = [scalars[0]] + [over_expert(scalars[q], shift_x(q)) for q in range(1, nx)]
        back = jnp.stack(back).reshape(nx, nz, cap)
        home = [back[:, 0]] + [over_expert(back[:, r], shift_z(-r)) for r in range(1, nz)]
        home = jnp.stack(home).reshape(n_expert, cap)
        far_z = (z + jnp.arange(nz, dtype=jnp.int32)) % nz
        far_x = (x - jnp.arange(nx, dtype=jnp.int32)) % nx
        ids = (far_z[:, None] * nx + far_x[None, :]).reshape(-1)
        mine, said = slots_of(routes.T, ids)
        by_token = jnp.sum(jnp.where(mine, home[:, :, None], 0.0), axis=1)
        gate_grad = jnp.sum(jnp.where(said, by_token[:, None], 0.0), axis=0).T / gate_prob
        return (
            jnp.concatenate(combined, axis=1),
            gate_grad,
            out,
            jnp.concatenate(weight_grad, axis=1)[None],
        )

    return local


def nothing(*refs):
    pass


def after(x, *deps):
    anywhere = pl.BlockSpec(memory_space=pl.ANY)
    return pl.pallas_call(
        nothing,
        out_shape=jax.ShapeDtypeStruct(x.shape, x.dtype),
        in_specs=[anywhere] * (1 + len(deps)),
        out_specs=anywhere,
        input_output_aliases={0: 0},
        name="after",
    )(x, *deps)


def call(kernel, grid, ins, outs, scratch, scalars, deps, cost):
    n_in, n_dep = len(ins), len(deps)
    n_scalar = 0 if scalars is None else 1

    def body(*refs):
        first, end = n_scalar + n_in, n_scalar + n_in + n_dep + len(outs) - 1
        refs[end][...] = jnp.zeros((8, 128), F32)
        kernel(*refs[:first], *refs[first + n_dep:end], *refs[end + 1:])

    outs = list(outs) + [((8, 128), F32, (8, 128), lambda *_: (0, 0))]

    specs = [pl.BlockSpec(block, index) for _, block, index in ins]
    specs += [pl.BlockSpec(memory_space=pl.ANY)] * n_dep
    return pl.pallas_call(
        body,
        out_shape=[jax.ShapeDtypeStruct(shape, dtype) for shape, dtype, _, _ in outs],
        grid_spec=pltpu.PrefetchScalarGridSpec(
            num_scalar_prefetch=n_scalar,
            grid=grid,
            in_specs=specs,
            out_specs=[pl.BlockSpec(block, index) for _, _, block, index in outs],
            scratch_shapes=list(scratch),
        ),
        compiler_params=pltpu.CompilerParams(vmem_limit_bytes=LIMITS.get(kernel.__name__, LIMIT) << 20),
        cost_estimate=pl.CostEstimate(flops=cost, bytes_accessed=cost // 300, transcendentals=0),
        name=kernel.__name__,
    )(*([] if scalars is None else [scalars]), *[a for a, _, _ in ins], *deps)


def build_tree(n_dp, n_expert):
    nz, nx, nc, ny = 4, 2, 2, 2

    def along_z(pairs):
        return [(a * nx + x, b * nx + x) for a, b in pairs for x in range(nx)]

    buddy = along_z([(0, 1), (1, 0), (2, 3), (3, 2)])
    middle = along_z([(1, 2), (2, 1)])
    skip = along_z([(0, 2), (2, 0), (1, 3), (3, 1)])
    mirror = along_z([(0, 3), (3, 0), (1, 2), (2, 1)])
    inward = along_z([(0, 1), (3, 2)])
    outward = along_z([(1, 0), (2, 3)])
    swap_x = [(e, e ^ 1) for e in range(n_expert)]
    swap_core = [(d, d ^ 1) for d in range(n_dp)]
    swap_y = [(d, d ^ 2) for d in range(n_dp)]

    def over_expert(a, pairs):
        return lax.ppermute(a, "expert", pairs)

    def over_dp(a, pairs):
        return lax.ppermute(a, "dp", pairs)

    def local(hidden_in, down_weight, routes, gate_prob, cotangent):
        me = lax.axis_index("expert")
        z, x = me // nx, me % nx
        dp = lax.axis_index("dp")
        cap = hidden_in.shape[2] // n_expert
        ff = hidden_in.shape[3]
        tok, top = routes.shape
        features = down_weight.shape[2]
        tile = 512
        tiles = features // tile
        first = (tiles + 1) // 2
        begin, count = (0, first), (first, tiles - first)
        widths = [n * tile for n in count]
        spans = [(b * tile, (b + n) * tile) for b, n in zip(begin, count)]
        half = 2 * cap
        part = ff // n_dp
        last, named = [], []

        def chain(kernel, grid, ins, outs, scratch=(), deps=(), flops=0):
            named.append(kernel.__name__)
            cost = COSTS.get(f"{named[-1]}{named.count(named[-1])}", COST)
            got = call(kernel, grid, ins, outs, scratch, scalars, tuple(last) + tuple(deps), cost)
            last[:] = got[-1:]
            return got[:-1]

        def hold(a, *deps):
            a = after(a, *last, *deps)
            last[:] = [a]
            return a
        blocks_in = hidden_in.reshape(n_expert, cap, ff)
        is_middle = (z == 1) | (z == 2)
        low = z < 2
        order_z = jnp.stack([z, z ^ 1, jnp.where(low, 2, 1), jnp.where(low, 3, 0)])
        order_x = jnp.stack([x, x ^ 1])
        order = (order_z[None, :] * nx + order_x[:, None]).reshape(-1)
        parts = jnp.stack([dp ^ 3, dp ^ 1, dp ^ 2, dp])
        scalars = jnp.concatenate(
            [order, parts, jnp.stack([is_middle.astype(jnp.int32), z * nx + x, z * nx + (x ^ 1)])]
        ).astype(jnp.int32)
        at_parts, at_middle, at_here = n_expert, n_expert + n_dp, n_expert + n_dp + 1

        buddies = over_expert(cotangent, buddy)
        mids = over_expert(cotangent, middle)
        table = jnp.concatenate([routes.astype(F32), gate_prob], axis=1).T

        def whole(a):
            return (a, a.shape, lambda *_: (0,) * a.ndim)

        def sliced(body, fixed):
            def run(s, *refs):
                kept, moving = refs[:fixed], refs[fixed:]
                for k in range(moving[-1].shape[-1] // tile):
                    body(s, *kept, *(ref.at[:, k * tile:(k + 1) * tile] for ref in moving))

            run.__name__ = body.__name__
            return run

        def strip_of(a):
            return (a, a.shape, lambda *_: (0, 0))

        def strip_out(rows, c, dtype=BF16):
            return ((rows, widths[c]), dtype, (rows, widths[c]), lambda *_: (0, 0))

        def columns(a, first=0):
            return (a, (a.shape[0], tile), lambda j, *_: (0, first + j))

        def wide(rows, c, dtype=BF16):
            return ((rows, widths[c]), dtype, (rows, tile), lambda j, *_: (0, j))

        def full(rows, dtype=BF16):
            return ((rows, features), dtype, (rows, tile), lambda j, *_: (0, j))

        broad = features // 4

        def broadly(rows):
            return ((rows, features), BF16, (rows, broad), lambda j, *_: (0, j))

        def product(q):
            def made(s, *refs):
                *given, w, w_low, near_ref, far_ref, rows = refs

                @pl.when(pl.program_id(0) == 0)
                def _():
                    for i, ref in enumerate(given):
                        rows[i * cap:(i + 1) * cap] = ref[0]

                middle_row = ff // 2
                out = dot(rows[:, :middle_row], w[0]) + dot(rows[:, middle_row:], w_low[0])
                near_ref[...] = out[:half].astype(BF16)
                far_ref[...] = out[half:].astype(BF16)

            ins = [
                (blocks_in, (1, cap, ff), lambda j, s, i=i: (s[q * nz + i], 0, 0)) for i in range(nz)
            ]
            for r in range(2):
                ins.append((down_weight, (1, ff // 2, broad), lambda j, s, r=r: (0, r, j)))
            return chain(
                made, (features // broad,), ins, [broadly(half), broadly(half)],
                [pltpu.VMEM((nz * cap, ff), BF16)],
            )

        there_near, there_far = product(1)
        pair = jnp.concatenate([table, over_expert(table, buddy)])
        rs_far = over_expert(there_far, swap_x)

        here_near, here_far = product(0)
        pair = hold(pair)
        far_pair = over_expert(pair, skip)

        def onehot(pos_ref, row):
            slot = lax.broadcasted_iota(jnp.int32, (cap, tok), 0)
            return slot == pos_ref[row:row + 1, :]

        def pack_rows(pos_ref, gate_ref, first, held, send_ref, keep_ref):
            for i, block in enumerate(held):
                for q, ref in enumerate((keep_ref, send_ref)):
                    row = (first + i) * nx + q
                    hot = onehot(pos_ref, row)
                    scale = jnp.sum(
                        jnp.where(hot, gate_ref[row:row + 1, :], 0.0), axis=1, keepdims=True
                    )
                    rows = dot(hot.astype(BF16), block)
                    ref[i * cap:(i + 1) * cap] = (rows * scale).astype(BF16)

        def spread_rows(pos_ref, gate_ref, row, here, there):
            total = None
            for q, rows in enumerate((here, there)):
                at = row * nx + q
                weighted = jnp.where(onehot(pos_ref, at), gate_ref[at:at + 1, :], 0.0).astype(BF16)
                term = lax.dot_general(
                    weighted, rows, (((0,), (0,)), ((), ())), preferred_element_type=F32
                )
                total = term if total is None else total + term
            return total

        def entire(rows, dtype=BF16, cols=None):
            shape = (rows, features if cols is None else cols)
            return (shape, dtype, shape, lambda *_: (0, 0))

        def packed_near(s, pos_ref, gate_ref, own, other, send_ref, keep_ref):
            pack_rows(pos_ref, gate_ref, 0, (own[...], other[...]), send_ref, keep_ref)

        def packed_far(s, pos_ref, gate_ref, m0, o0, m1, o1, first_ref, second_ref, keep_ref):
            middle_here = s[at_middle] == 1
            for k in range(tiles):
                at = slice(k * tile, (k + 1) * tile)
                held = [
                    jnp.where(middle_here, a[:, at], b[:, at]) for a, b in ((m0, o0), (m1, o1))
                ]
                send, moved = (first_ref, 0) if k < first else (second_ref, first)
                send = send.at[:, (k - moved) * tile:(k - moved + 1) * tile]
                pack_rows(pos_ref, gate_ref, 2, held, send, keep_ref.at[:, at])

        def shared_far(s, pos_ref, gate_ref, here, there, far_ref, last_ref):
            for i, ref in enumerate((far_ref, last_ref)):
                lines = slice(i * cap, (i + 1) * cap)
                total = spread_rows(pos_ref, gate_ref, 2 + i, here[lines], there[lines])
                ref[...] = total.astype(BF16)

        def shared_near(s, pos_ref, gate_ref, here, there, sum_ref, keep_ref, send_ref):
            for i, ref in enumerate((keep_ref, send_ref)):
                lines = slice(i * cap, (i + 1) * cap)
                total = spread_rows(pos_ref, gate_ref, i, here[lines], there[lines])
                if i == 1:
                    total = total + sum_ref[...].astype(F32)
                ref[...] = total.astype(ref.dtype)

        def plus(a, b):
            def add(s, a_ref, b_ref, out_ref):
                out_ref[...] = a_ref[...] + b_ref[...]

            return chain(add, (1,), [whole(a), whole(b)], [entire(tok)])[0]

        def turned(s, *refs):
            *given, out_ref, rows = refs

            @pl.when(pl.program_id(0) == 0)
            def _():
                for i, ref in enumerate(given):
                    rows[i * cap:(i + 1) * cap] = ref[0]

            first = pl.multiple_of(s[at_parts + pl.program_id(0)] * part, part)
            out_ref[...] = rows[:, pl.ds(first, part)].T

        slots = n_expert * cap

        buddies = hold(buddies)
        mid_last = over_expert(buddies, middle)
        mids = hold(mids)
        out_far = over_expert(mids, outward)

        def positions(s, near_ref, far_ref, pos_ref, gate_ref):
            middle_here = s[at_middle] == 1
            rows = 2 * top
            held = [
                near_ref[:rows],
                near_ref[rows:],
                jnp.where(middle_here, far_ref[rows:], far_ref[:rows]),
                jnp.where(middle_here, far_ref[:rows], far_ref[rows:]),
            ]
            match, gates = [], []
            for t in held:
                for q in range(nx):
                    named = t[:top] == s[at_here + q].astype(F32)
                    match.append(jnp.sum(named.astype(F32), axis=0, keepdims=True))
                    gates.append(jnp.sum(jnp.where(named, t[top:], 0.0), axis=0, keepdims=True))
            match = jnp.concatenate(match, axis=0)
            earlier = lax.broadcasted_iota(jnp.int32, (tok, tok), 0) < lax.broadcasted_iota(
                jnp.int32, (tok, tok), 1
            )
            before = dot(match.astype(BF16), earlier.astype(BF16))
            pos_ref[...] = jnp.where(match > 0, before, -1.0).astype(jnp.int32)
            gate_ref[...] = jnp.concatenate(gates, axis=0)

        small = (nz * nx, tok)
        pos, gate = chain(
            positions, (1,), [whole(pair), whole(far_pair)],
            [(small, jnp.int32, small, lambda *_: (0, 0)), (small, F32, small, lambda *_: (0, 0))],
        )
        def pieces(c):
            whole_width = [columns(a, begin[c]) for a in (own_near, own_far, ag_near)]
            return whole_width + [columns(ag_far[c])]

        share_rows = ny * part

        def stack_pieces(given, rows):
            for i, ref in enumerate(given):
                rows[i * half:(i + 1) * half] = ref[...]

        def weight_give(c):
            def gave(s, *refs):
                *given, turned_ref, out_ref, rows_ref = refs
                stack_pieces(given, rows_ref)
                out_ref[...] = dot(turned_ref[...], rows_ref[...]).astype(BF16)

            return chain(
                gave, (count[c],),
                pieces(c) + [(hidden_t, (share_rows, slots), lambda *_: (0, 0))],
                [wide(share_rows, c), wide(slots, c)],
            )

        def weight_keep(rows, c, got):
            def kept(s, rows_ref, turned_ref, got_ref, send_ref, keep_ref):
                out = dot(turned_ref[...], rows_ref[...]).astype(BF16).astype(F32)
                out = out + got_ref[...].astype(F32)
                send_ref[...] = out[:part].astype(BF16)
                keep_ref[...] = out[part:]

            return chain(
                kept, (count[c],),
                [columns(rows), (hidden_t, (share_rows, slots), lambda *_: (1, 0)), columns(got)],
                [wide(part, c), wide(part, c, F32)],
            )

        def hidden_all(rows_a, rows_b, deps):
            strip = 256

            def hidden(s, a_ref, b_ref, w, h, out_ref, scalar_ref):
                j = pl.program_id(0)
                total = None
                for ref, (first, end) in zip((a_ref, b_ref), spans):
                    term = lax.dot_general(
                        ref[...], w[0, :, first:end], (((1,), (1,)), ((), ())),
                        preferred_element_type=F32,
                    )
                    total = term if total is None else total + term
                for i in range(n_expert):
                    mine = total[i * cap:(i + 1) * cap]
                    out_ref[s[i]] = mine.astype(BF16)
                    term = jnp.sum(mine * h[s[i]].astype(F32), axis=1, keepdims=True)
                    term = jnp.broadcast_to(term, (cap, 128))

                    @pl.when(j == 0)
                    def _():
                        scalar_ref[i] = term

                    @pl.when(j > 0)
                    def _():
                        scalar_ref[i] += term

            strips = (n_expert, cap, strip)
            return chain(
                hidden, (ff // strip,),
                [
                    whole(rows_a), whole(rows_b),
                    (down_weight, (1, strip, features), lambda j, s: (0, j, 0)),
                    (blocks_in, strips, lambda j, s: (0, 0, j)),
                ],
                [
                    (blocks_in.shape, BF16, strips, lambda j, s: (0, 0, j)),
                    ((n_expert, cap, 128), F32, (n_expert, cap, 128), lambda *_: (0, 0, 0)),
                ],
                (), deps,
            )

        there_near = hold(there_near)
        send, own_near = chain(
            sliced(packed_near, 2), (1,),
            [whole(a) for a in (pos, gate, cotangent, buddies)], [entire(half), entire(half)],
        )
        ag_near = over_expert(send, swap_x)
        rs_near = over_expert(there_near, swap_x)
        (hidden_t,) = chain(
            turned, (n_dp,),
            [(blocks_in, (1, cap, ff), lambda j, s, i=i: (s[i], 0, 0)) for i in range(n_expert)],
            [((ff, slots), BF16, (part, slots), lambda j, *_: (j, 0))],
            [pltpu.VMEM((slots, ff), BF16)],
        )
        sum_far, sum_last = chain(
            sliced(shared_far, 2), (1,),
            [whole(a) for a in (pos, gate, here_far, rs_far)],
            [entire(tok), entire(tok)],
        )
        one = over_expert(sum_last, inward)
        mid_last = hold(mid_last, out_far)
        out_last = over_expert(mid_last, outward)
        rs_near = hold(rs_near)
        two = over_expert(plus(sum_last, one), middle)
        sum_far = hold(sum_far, one)
        one_far = over_expert(sum_far, inward)
        send_a, send_b, own_far = chain(
            packed_far, (1,),
            [whole(a) for a in (pos, gate, mids, out_far, mid_last, out_last)],
            [entire(half, BF16, widths[0]), entire(half, BF16, widths[1]), entire(half)],
        )
        ag_far = [over_expert(send_a, swap_x), over_expert(send_b, swap_x)]
        two_far = over_expert(plus(sum_far, one_far), middle)
        give, rows_a = weight_give(0)
        got = over_dp(give, swap_core)
        keep, give = chain(
            sliced(shared_near, 2), (1,),
            [whole(a) for a in (pos, gate, here_near, rs_near, two)],
            [entire(tok, F32), entire(tok)],
        )
        three = over_expert(give, buddy)
        send_a, keep_a = weight_keep(rows_a, 0, got)
        got_a = over_dp(send_a, swap_y)
        give, rows_b = weight_give(1)
        got = over_dp(give, swap_core)
        hidden_grad, scalar_rows = hidden_all(rows_a, rows_b, ())
        two_far = hold(two_far)
        send_b, keep_b = weight_keep(rows_b, 1, got)
        got_b = over_dp(send_b, swap_y)
        scalar_rows = hold(scalar_rows)
        three = hold(three)
        got_a = hold(got_a)

        def add_three(s, a, b, c, out_ref):
            total = a[...] + b[...].astype(F32) + c[...].astype(F32)
            out_ref[...] = total.astype(BF16)

        (combined,) = chain(
            add_three, (1,), [whole(a) for a in (keep, three, two_far)], [entire(tok)]
        )

        def add_chunks(s, *refs):
            *given, out_ref = refs
            for c in range(2):
                total = given[2 * c][...] + given[2 * c + 1][...].astype(F32)
                out_ref[0, :, spans[c][0]:spans[c][1]] = total.astype(BF16)

        strip = part // 2
        (weight_grad,) = chain(
            add_chunks, (2,),
            [(a, (strip, a.shape[1]), lambda j, *_: (j, 0)) for a in (keep_a, got_a, keep_b, got_b)],
            [((1, part, features), BF16, (1, strip, features), lambda j, *_: (0, j, 0))],
        )

        back = scalar_rows[:, :, 0].reshape(nx, nz, cap)
        back = jnp.stack([back[0], over_expert(back[1], swap_x)], axis=1)
        home = jnp.stack(
            [
                back[0],
                over_expert(back[1], buddy),
                over_expert(jnp.where(is_middle, back[3], back[2]), skip),
                over_expert(jnp.where(is_middle, back[2], back[3]), mirror),
            ]
        ).reshape(n_expert, cap)
        from_z = jnp.stack([z, z ^ 1, z ^ 2, 3 - z])
        ids = (from_z[:, None] * nx + order_x[None, :]).reshape(-1)
        said = routes.T[None] == ids[:, None, None]
        match = said.any(axis=1)
        count = match.astype(jnp.int32)
        before = jnp.cumsum(count, axis=1) - count
        slot = jnp.arange(cap, dtype=jnp.int32)[:, None]
        mine = match[:, None, :] & (before[:, None, :] == slot)
        by_token = jnp.sum(jnp.where(mine, home[:, :, None], 0.0), axis=1)
        gate_grad = jnp.sum(jnp.where(said, by_token[:, None], 0.0), axis=0).T / gate_prob
        return (
            combined,
            gate_grad,
            hidden_grad.reshape(hidden_in.shape),
            weight_grad,
        )

    return local


def build(n_dp, n_expert):
    if split_expert(n_expert) == (4, 2) and n_dp == 4:
        return build_tree(n_dp, n_expert)
    return build_line(n_dp, n_expert)


def solution(mesh):
    in_specs = (
        P("expert", "dp", None, None),
        P("expert", None, None),
        P(("dp", "expert"), None),
        P(("dp", "expert"), None),
        P(("dp", "expert"), None),
    )
    out_specs = (
        P(("dp", "expert"), None),
        P(("dp", "expert"), None),
        P("expert", "dp", None, None),
        P("expert", "dp", None),
    )
    local = build(mesh.shape["dp"], mesh.shape["expert"])
    return jax.shard_map(local, mesh=mesh, in_specs=in_specs, out_specs=out_specs, check_vma=False)
```
